256 devices in a mesh: dp: 32 (over z, y), expert: 8 (over x, core).
Axes of the slice: x: 4, y: 4, z: 8, core: 2. Of those that a mesh axis runs over, the one named last changes fastest.
Arguments:
- tokens: bfloat16 [4096, 2048], P(('dp', 'expert')), may hold values from -6 to 6
- expert_ids: int32 [4096, 8], P(('dp', 'expert')), may hold values from 0 to 127, as said below
- route_weight: float32 [4096, 8], P(('dp', 'expert')), may hold values from 0.03 to 0.6
- out_grad: bfloat16 [4096, 2048], P(('dp', 'expert')), may hold values from -6 to 6
- gate_weight: bfloat16 [256, 2048, 384], P(('dp', 'expert')), may hold values from -0.125 to 0.125
- up_weight: bfloat16 [256, 2048, 384], P(('dp', 'expert')), may hold values from -0.125 to 0.125
- down_weight: bfloat16 [256, 384, 2048], P(('dp', 'expert')), may hold values from -0.21875 to 0.21875
Outputs:
- layer_out: bfloat16 [4096, 2048], P(('dp', 'expert'))
- token_grad: bfloat16 [4096, 2048], P(('dp', 'expert'))
- route_grad: float32 [4096, 8], P(('dp', 'expert'))
- gate_grad: bfloat16 [256, 2048, 384], P(('dp', 'expert'))
- up_grad: bfloat16 [256, 2048, 384], P(('dp', 'expert'))
- down_grad: bfloat16 [256, 384, 2048], P(('dp', 'expert'))
The draws below stay inside these ranges and needn't reach their ends.
Inputs may be any that keep to these rules, and one draw needn't show every extreme that they name: `expert_ids`: each row names 8 different experts. The rows of one device name no expert more than 2 times, and one expert is named exactly 2 times by the rows of every device.
All inputs are finite; a program needn't handle non-finite values.
Results may differ from the reference program's by a relative error of at most 0.0071.
Values may be sent and summed in bfloat16 or wider, within the bound.
No kernel may reach another device: no remote copies, remote signals or barrier semaphores. Data moves between devices by JAX's collectives and lax.ppermute only.
A program may use at most 128 MiB of HBM per device.

```python
import math
import jax
import jax.numpy as jnp
from jax import lax

D = 2048
FF = 768
TOP = 8
TOK_DEV = 16
HALF = 384
EXPERTS = 128
CAP = 2
TOKENS = 4096
DEVICES = 256


def shuffle_experts(subkey):
    return jax.random.permutation(subkey, EXPERTS - 1)


def shuffle_rows(subkey):
    return jax.random.permutation(subkey, TOK_DEV)


def draw_expert_ids(key, part):
    base_key = jax.random.fold_in(key, 7)
    key_hot, key_width, key_perm, key_rows, key_turn = jax.random.split(base_key, 5)
    blocks = TOKENS // TOK_DEV
    hot_expert = jax.random.randint(key_hot, (), 0, EXPERTS)
    widths = jax.random.randint(key_width, (blocks,), EXPERTS // 2, EXPERTS)
    orders = jax.vmap(shuffle_experts)(jax.random.split(key_perm, blocks))
    others = orders + (orders >= hot_expert).astype(jnp.int32)
    row_ids = jnp.arange(TOK_DEV, dtype=jnp.int32)[:, None]
    pick_ids = jnp.arange(TOP, dtype=jnp.int32)[None, :]
    hot_slot = (row_ids < CAP) & (pick_ids == 0)
    earlier = jnp.minimum(row_ids, CAP) + ((row_ids < CAP) & (pick_ids > 0)).astype(jnp.int32)
    running = row_ids * TOP + pick_ids - earlier
    position = running[None, :, :] % widths[:, None, None]
    chosen = jnp.take_along_axis(others, position.reshape(blocks, TOK_DEV * TOP), axis=1).reshape(blocks, TOK_DEV, TOP)
    routed = jnp.where(hot_slot[None, :, :], hot_expert, chosen)
    row_perm = jax.vmap(shuffle_rows)(jax.random.split(key_rows, blocks))
    routed = jnp.take_along_axis(routed, row_perm[:, :, None], axis=1)
    rotation = jax.random.randint(key_turn, (blocks, TOK_DEV, 1), 0, TOP)
    routed = jnp.take_along_axis(routed, (pick_ids[None, :, :] + rotation) % TOP, axis=2)
    return routed.reshape(TOKENS, TOP).astype(jnp.int32)


def block_levels(key, extent, cuts, least, largest):
    gain = 1.0
    for axis_at, parts in cuts:
        heights = jax.random.uniform(jax.random.fold_in(jax.random.fold_in(key, 6), axis_at), (parts,), jnp.float32, least / len(cuts), largest / len(cuts))
        gain = gain * jnp.repeat(jnp.exp(heights), extent[axis_at] // parts).reshape((-1,) + (1,) * (len(extent) - 1 - axis_at))
    return gain


def noise(own_key, dims, deviation, limit, cuts=(), kind=jnp.bfloat16):
    entries = jax.random.normal(own_key, dims, jnp.float32) * deviation
    if len(cuts) > 0:
        entries = block_levels(own_key, dims, cuts, -0.22, 0.18) * entries
    return jnp.clip(entries, min=-limit, max=limit).astype(kind)


def setup_inputs(seed: int = 0) -> dict:
    key_of = jax.random.split(jax.random.key(seed), 8)
    tokens = noise(key_of[0], (TOKENS, D), 1.0, 6.0, ((0, 256),))
    expert_ids = draw_expert_ids(jax.random.fold_in(key_of[7], 71), 0)
    route_weight = jnp.clip(jnp.exp(math.log(0.6) - 2.9957323 * jax.random.uniform(key_of[2], (TOKENS, TOP), jnp.float32) ** block_levels(key_of[2], (TOKENS, TOP), ((0, 256),), -0.2, 0.2)), 0.03, 0.6)
    out_grad = noise(key_of[3], (TOKENS, D), 1.0, 6.0, ((0, 256),))
    gate_weight = noise(key_of[4], (DEVICES, D, HALF), D ** -0.5, 0.125, ((0, 256),))
    up_weight = noise(key_of[5], (DEVICES, D, HALF), D ** -0.5, 0.125, ((0, 256),))
    down_weight = noise(key_of[6], (DEVICES, HALF, D), FF ** -0.5, 0.21875, ((0, 256),))
    return dict(tokens=tokens, expert_ids=expert_ids, route_weight=route_weight, out_grad=out_grad, gate_weight=gate_weight, up_weight=up_weight, down_weight=down_weight)


def reference(tokens, expert_ids, route_weight, out_grad, gate_weight, up_weight, down_weight):
    tok_total = tokens.shape[0]
    assigned = tok_total * TOP
    flat_ids = expert_ids.reshape(-1).astype(jnp.int32)
    per_block = flat_ids.reshape(-1, TOK_DEV * TOP)
    onehot = (per_block[:, :, None] == jnp.arange(EXPERTS, dtype=jnp.int32)[None, None, :]).astype(jnp.int32)
    before = jnp.cumsum(onehot, axis=1) - onehot
    slot_ids = jnp.sum(before * onehot, axis=2).reshape(-1).astype(jnp.int32)
    device_ids = jnp.arange(assigned, dtype=jnp.int32) // (TOK_DEV * TOP)
    place_row = ((flat_ids * DEVICES + device_ids) * CAP + slot_ids).astype(jnp.int32)
    slot_table = jnp.full((EXPERTS * DEVICES * CAP,), -1, jnp.int32).at[place_row].set(jnp.arange(assigned, dtype=jnp.int32))
    slot_table = slot_table.reshape(EXPERTS, DEVICES * CAP)
    weights_flat = route_weight.reshape(-1)

    def expert_step(accum, expert):
        out_acc, grad_acc, route_acc = accum
        entry_ids = slot_table[expert]
        filled = entry_ids >= 0
        assign = jnp.maximum(entry_ids, 0)
        tok_rows = assign // TOP
        in_rows = jnp.where(filled[:, None], tokens[tok_rows], jnp.zeros((), jnp.bfloat16))
        weight_rows = jnp.where(filled, weights_flat[assign], jnp.zeros((), jnp.float32))
        grad_rows = out_grad[tok_rows].astype(jnp.float32)
        scaled = (weight_rows[:, None] * grad_rows).astype(jnp.bfloat16)
        partials = []
        partial_grads = []
        gate_pieces = []
        up_pieces = []
        down_pieces = []
        for piece_half in range(2):
            piece_id = 2 * expert + piece_half
            w_gate = gate_weight[piece_id]
            w_up = up_weight[piece_id]
            w_down = down_weight[piece_id]
            gate_act = jnp.dot(in_rows, w_gate, preferred_element_type=jnp.float32)
            up_act = jnp.dot(in_rows, w_up, preferred_element_type=jnp.float32)
            sig_gate = jax.nn.sigmoid(gate_act)
            hidden = (gate_act * sig_gate * up_act).astype(jnp.bfloat16)
            partials.append(jnp.dot(hidden, w_down, preferred_element_type=jnp.float32).astype(jnp.bfloat16))
            hidden_grad = jnp.dot(scaled, w_down.T, preferred_element_type=jnp.float32)
            gate_pre = (hidden_grad * up_act * sig_gate * (1.0 + gate_act * (1.0 - sig_gate))).astype(jnp.bfloat16)
            up_pre = (hidden_grad * gate_act * sig_gate).astype(jnp.bfloat16)
            partial_grads.append((jnp.dot(gate_pre, w_gate.T, preferred_element_type=jnp.float32) + jnp.dot(up_pre, w_up.T, preferred_element_type=jnp.float32)).astype(jnp.bfloat16))
            gate_pieces.append(jnp.dot(in_rows.T, gate_pre, preferred_element_type=jnp.float32).astype(jnp.bfloat16))
            up_pieces.append(jnp.dot(in_rows.T, up_pre, preferred_element_type=jnp.float32).astype(jnp.bfloat16))
            down_pieces.append(jnp.dot(hidden.T, scaled, preferred_element_type=jnp.float32).astype(jnp.bfloat16))
        expert_out = (partials[0].astype(jnp.float32) + partials[1].astype(jnp.float32)).astype(jnp.bfloat16)
        out_acc = out_acc.at[tok_rows].add(weight_rows[:, None] * expert_out.astype(jnp.float32))
        route_term = jnp.sum(grad_rows * expert_out.astype(jnp.float32), axis=1)
        route_acc = route_acc.at[assign].add(jnp.where(filled, route_term, jnp.zeros((), jnp.float32)))
        expert_grad = (partial_grads[0].astype(jnp.float32) + partial_grads[1].astype(jnp.float32)).astype(jnp.bfloat16)
        grad_acc = grad_acc.at[tok_rows].add(jnp.where(filled[:, None], expert_grad.astype(jnp.float32), jnp.zeros((), jnp.float32)))
        return (out_acc, grad_acc, route_acc), (jnp.stack(gate_pieces), jnp.stack(up_pieces), jnp.stack(down_pieces))

    start = (jnp.zeros((tok_total, D), jnp.float32), jnp.zeros((tok_total, D), jnp.float32), jnp.zeros((assigned,), jnp.float32))
    final, stacked = lax.scan(expert_step, start, jnp.arange(EXPERTS, dtype=jnp.int32))
    out_acc, grad_acc, route_acc = final
    gate_all, up_all, down_all = stacked
    return (out_acc.astype(jnp.bfloat16), grad_acc.astype(jnp.bfloat16), route_acc.reshape(tok_total, TOP),
            gate_all.reshape(DEVICES, D, HALF), up_all.reshape(DEVICES, D, HALF), down_all.reshape(DEVICES, HALF, D))
```

```python
import functools

import jax
import jax.numpy as jnp
from jax import lax
from jax.experimental import pallas as pl
from jax.experimental.pallas import tpu as pltpu
from jax.sharding import Mesh, PartitionSpec as P

AXES = ("z", "y", "x", "core")
SIZES = (8, 4, 4, 2)
PLANES = 8
CHIPS = 16
TOK = 16
TOP = 8
SLOTS = 2
D = 2048
HALF = 384
META = 128
COLS = 2 * D + META
GROUP = PLANES * TOK
ROWS = CHIPS * PLANES * SLOTS
F32 = jnp.float32
BF16 = jnp.bfloat16
VMEM = pl.BlockSpec(memory_space=pltpu.VMEM)
SMEM = pl.BlockSpec(memory_space=pltpu.SMEM)


def params(mib):
    return pltpu.CompilerParams(vmem_limit_bytes=mib * 2**20)


def dot(a, b, a_dim, b_dim):
    return lax.dot_general(a, b, (((a_dim,), (b_dim,)), ((), ())), preferred_element_type=F32)


def three_pieces(value):
    high = value.astype(BF16)
    rest = value - high.astype(F32)
    middle = rest.astype(BF16)
    low = (rest - middle.astype(F32)).astype(BF16)
    return high, middle, low


def pack_kernel(tok_ref, grad_ref, ids_ref, weight_ref, out_ref):
    pieces = (ids_ref[...].astype(F32).astype(BF16),) + three_pieces(weight_ref[...])
    rows = lax.broadcasted_iota(jnp.int32, (TOP, META), 0)
    lanes = lax.broadcasted_iota(jnp.int32, (TOP, META), 1)
    meta = jnp.zeros((TOK, META), F32)
    for i, piece in enumerate(pieces):
        place = jnp.where(lanes == rows + i * TOP, 1.0, 0.0).astype(BF16)
        meta = meta + dot(piece, place, 0, 0)
    meta = meta.astype(BF16)
    for z in range(PLANES):
        out_ref[z, :, :D] = tok_ref[...]
        out_ref[z, :, D : 2 * D] = grad_ref[...]
        out_ref[z, :, 2 * D :] = meta


def pack(tokens, out_grad, ids_t, weight_t):
    return pl.pallas_call(
        pack_kernel,
        out_shape=jax.ShapeDtypeStruct((PLANES, TOK, COLS), BF16),
        in_specs=[VMEM] * 4,
        out_specs=VMEM,
        compiler_params=params(16),
        name="pack_rows",
    )(tokens, out_grad, ids_t, weight_t)


def spread_kernel(first_ref, all_ref, send_ref, mask_ref, weight_ref):
    meta = all_ref[:, 2 * D :].astype(F32)
    shape = (GROUP, ROWS)
    lane = lax.broadcasted_iota(jnp.int32, shape, 1)
    row = lax.broadcasted_iota(jnp.int32, shape, 0)
    expert = (first_ref[0] + lane // (PLANES * SLOTS)).astype(F32)
    named = jnp.zeros(shape, F32)
    weight = jnp.zeros(shape, F32)
    for k in range(TOP):
        hit = meta[:, k : k + 1] == expert
        w = meta[:, TOP + k : TOP + k + 1] + meta[:, 2 * TOP + k : 2 * TOP + k + 1]
        w = w + meta[:, 3 * TOP + k : 3 * TOP + k + 1]
        named = jnp.where(hit, 1.0, named)
        weight = jnp.where(hit, w, weight)
    ri = lax.broadcasted_iota(jnp.int32, (GROUP, GROUP), 0)
    ci = lax.broadcasted_iota(jnp.int32, (GROUP, GROUP), 1)
    earlier = jnp.where((ri // TOK == ci // TOK) & (ci < ri), 1.0, 0.0).astype(BF16)
    slot = dot(earlier, named.astype(BF16), 1, 0)
    wanted = (lane % SLOTS).astype(F32)
    source = (lane // SLOTS) % PLANES
    mask = jnp.where((slot == wanted) & (source == row // TOK), named, 0.0)
    weight = weight * mask
    mask_ref[...] = mask.astype(BF16)
    weight_ref[...] = weight
    pick = mask.T.astype(BF16)
    scale = jnp.sum(weight.T, axis=1, keepdims=True)
    for i in range(0, D, 512):
        send_ref[:, i : i + 512] = dot(pick, all_ref[:, i : i + 512], 1, 0).astype(BF16)
    for i in range(D, 2 * D, 512):
        send_ref[:, i : i + 512] = (dot(pick, all_ref[:, i : i + 512], 1, 0) * scale).astype(BF16)


def spread(first, gathered):
    return pl.pallas_call(
        spread_kernel,
        out_shape=(
            jax.ShapeDtypeStruct((ROWS, 2 * D), BF16),
            jax.ShapeDtypeStruct((GROUP, ROWS), BF16),
            jax.ShapeDtypeStruct((GROUP, ROWS), F32),
        ),
        in_specs=[SMEM, VMEM],
        out_specs=(VMEM, VMEM, VMEM),
        compiler_params=params(24),
        name="spread_rows",
    )(first, gathered)


def expert_kernel(in_ref, gate_ref, up_ref, down_ref, back_ref, hidden_ref, pre_ref, up_pre_ref):
    w_gate = gate_ref[0]
    w_up = up_ref[0]
    w_down = down_ref[0]
    rows = in_ref[:, :D]
    gate = dot(rows, w_gate, 1, 0)
    up = dot(rows, w_up, 1, 0)
    sig = jax.nn.sigmoid(gate)
    act = gate * sig
    hidden = (act * up).astype(BF16)
    hidden_ref[...] = hidden
    hidden_grad = dot(in_ref[:, D:], w_down, 1, 1)
    pre = (hidden_grad * up * sig * (1.0 + gate * (1.0 - sig))).astype(BF16)
    up_pre = (hidden_grad * act).astype(BF16)
    pre_ref[...] = pre
    up_pre_ref[...] = up_pre
    for i in range(0, D, 512):
        back_ref[:, i : i + 512] = dot(hidden, down_ref[0, :, i : i + 512], 1, 0).astype(BF16)
    for i in range(0, D, 512):
        back_ref[:, D + i : D + i + 512] = (
            dot(pre, gate_ref[0, i : i + 512, :], 1, 1) + dot(up_pre, up_ref[0, i : i + 512, :], 1, 1)
        ).astype(BF16)


def expert(rows, gate_weight, up_weight, down_weight):
    act = jax.ShapeDtypeStruct((ROWS, HALF), BF16)
    return pl.pallas_call(
        expert_kernel,
        out_shape=(jax.ShapeDtypeStruct((ROWS, 2 * D), BF16), act, act, act),
        in_specs=[VMEM] * 4,
        out_specs=(VMEM,) * 4,
        compiler_params=params(40),
        cost_estimate=pl.CostEstimate(
            flops=12 * ROWS * D * HALF, bytes_accessed=8 * 2**20, transcendentals=ROWS * HALF
        ),
        name="expert_rows",
    )(rows, gate_weight, up_weight, down_weight)


def weight_grad_kernel(x_a, g_a, x_b, g_b, h_a, p_a, u_a, h_b, p_b, u_b, gate_ref, up_ref, down_ref):
    gate_ref[0] = (dot(x_a[...], p_a[...], 0, 0) + dot(x_b[...], p_b[...], 0, 0)).astype(BF16)
    up_ref[0] = (dot(x_a[...], u_a[...], 0, 0) + dot(x_b[...], u_b[...], 0, 0)).astype(BF16)
    down_ref[0] = (dot(h_a[...], g_a[...], 0, 0) + dot(h_b[...], g_b[...], 0, 0)).astype(BF16)


def weight_grads(own, other, own_acts, other_acts):
    width = 512
    steps = D // width
    x_spec = pl.BlockSpec((ROWS, width), lambda i: (0, i))
    g_spec = pl.BlockSpec((ROWS, width), lambda i: (0, i + steps))
    act_spec = pl.BlockSpec((ROWS, HALF), lambda i: (0, 0))
    wide = pl.BlockSpec((1, width, HALF), lambda i: (0, i, 0))
    return pl.pallas_call(
        weight_grad_kernel,
        grid=(steps,),
        out_shape=(
            jax.ShapeDtypeStruct((1, D, HALF), BF16),
            jax.ShapeDtypeStruct((1, D, HALF), BF16),
            jax.ShapeDtypeStruct((1, HALF, D), BF16),
        ),
        in_specs=[x_spec, g_spec, x_spec, g_spec] + [act_spec] * 6,
        out_specs=(wide, wide, pl.BlockSpec((1, HALF, width), lambda i: (0, 0, i))),
        compiler_params=params(32),
        cost_estimate=pl.CostEstimate(
            flops=12 * ROWS * D * HALF, bytes_accessed=12 * 2**20, transcendentals=0
        ),
        name="weight_grads",
    )(own, own, other, other, *own_acts, *other_acts)


def combine_kernel(first_ref, back_ref, all_ref, mask_ref, weight_ref, out_ref):
    mask = mask_ref[...]
    weight = weight_ref[...]
    high = weight.astype(BF16)
    low = (weight - high.astype(F32)).astype(BF16)
    products = jnp.zeros((GROUP, ROWS), F32)
    for i in range(0, D, 512):
        part = back_ref[:, i : i + 512]
        total = dot(high, part, 1, 0) + dot(low, part, 1, 0)
        out_ref[:, i : i + 512] = total.astype(BF16)
        products = products + dot(all_ref[:, D + i : D + i + 512], part, 1, 1)
    for i in range(D, 2 * D, 512):
        out_ref[:, i : i + 512] = dot(mask, back_ref[:, i : i + 512], 1, 0).astype(BF16)
    meta = all_ref[:, 2 * D :].astype(F32)
    products = products * mask.astype(F32)
    lane = lax.broadcasted_iota(jnp.int32, (GROUP, ROWS), 1)
    expert_of = (first_ref[0] + lane // (PLANES * SLOTS)).astype(F32)
    place = lax.broadcasted_iota(jnp.int32, (GROUP, META), 1)
    tail = jnp.zeros((GROUP, META), F32)
    for k in range(TOP):
        hit = meta[:, k : k + 1] == expert_of
        value = jnp.sum(jnp.where(hit, products, 0.0), axis=1, keepdims=True)
        for i, piece in enumerate(three_pieces(value)):
            tail = jnp.where(place == i * TOP + k, piece.astype(F32), tail)
    out_ref[:, 2 * D :] = tail.astype(BF16)


def combine(first, back, gathered, mask, weight):
    return pl.pallas_call(
        combine_kernel,
        out_shape=jax.ShapeDtypeStruct((GROUP, COLS), BF16),
        in_specs=[SMEM] + [VMEM] * 4,
        out_specs=VMEM,
        compiler_params=params(24),
        name="combine_rows",
    )(first, back, gathered, mask, weight)


def total_kernel(in_ref, out_ref, grad_ref, route_ref):
    total = in_ref[0].astype(F32)
    for z in range(1, PLANES):
        total = total + in_ref[z].astype(F32)
    out_ref[...] = total[:, :D].astype(BF16)
    grad_ref[...] = total[:, D : 2 * D].astype(BF16)
    tail = total[:, 2 * D :].T
    route_ref[...] = tail[:TOP] + tail[TOP : 2 * TOP] + tail[2 * TOP : 3 * TOP]


def totals(arrived):
    return pl.pallas_call(
        total_kernel,
        out_shape=(
            jax.ShapeDtypeStruct((TOK, D), BF16),
            jax.ShapeDtypeStruct((TOK, D), BF16),
            jax.ShapeDtypeStruct((TOP, TOK), F32),
        ),
        in_specs=[VMEM],
        out_specs=(VMEM, VMEM, VMEM),
        compiler_params=params(16),
        name="total_rows",
    )(arrived)


def swap_cores(value):
    return lax.ppermute(value, "core", [(0, 1), (1, 0)])


def over_plane(value):
    blocks = value.reshape(CHIPS, PLANES * SLOTS, 2 * D)
    return lax.all_to_all(blocks, ("y", "x"), 0, 0, tiled=True).reshape(ROWS, 2 * D)


def over_z(value):
    return lax.all_to_all(value, "z", 0, 0, tiled=True)


def body(tokens, expert_ids, route_weight, out_grad, gate_weight, up_weight, down_weight):
    first = (lax.axis_index("z") * CHIPS).astype(jnp.int32).reshape(1)
    gathered = over_z(pack(tokens, out_grad, expert_ids.T, route_weight.T)).reshape(GROUP, COLS)
    send, mask, weight = spread(first, gathered)
    own = over_plane(send)
    other = swap_cores(own)
    own_back, *own_acts = expert(own, gate_weight, up_weight, down_weight)
    other_back, *other_acts = expert(other, gate_weight, up_weight, down_weight)
    from_other = swap_cores(other_back)
    summed = (own_back.astype(F32) + from_other.astype(F32)).astype(BF16)
    back = over_plane(summed)
    gate_grad, up_grad, down_grad = weight_grads(own, other, own_acts, other_acts)
    partial = combine(first, back, gathered, mask, weight)
    layer_out, token_grad, route_t = totals(over_z(partial.reshape(PLANES, TOK, COLS)))
    return layer_out, token_grad, route_t.T, gate_grad, up_grad, down_grad


def solution(mesh):
    fine = Mesh(mesh.devices.reshape(SIZES), AXES)
    rows, pieces = P(AXES, None), P(AXES, None, None)
    return jax.shard_map(
        body,
        mesh=fine,
        in_specs=(rows, rows, rows, rows, pieces, pieces, pieces),
        out_specs=(rows, rows, rows, pieces, pieces, pieces),
        check_vma=False,
    )
```

```python
import functools

import jax
import jax.numpy as jnp
from jax import lax
from jax.experimental import pallas as pl
from jax.experimental.pallas import tpu as pltpu
from jax.sharding import Mesh, PartitionSpec as P

AXES = ("z", "y", "x", "core")
SIZES = (8, 4, 4, 2)
PLANES = 8
CHIPS = 16
TOK = 16
TOP = 8
SLOTS = 2
D = 2048
HALF = 384
META = 128
COLS = 2 * D + META
GROUP = PLANES * TOK
ROWS = CHIPS * PLANES * SLOTS
BLOCKS = PLANES + 1
F32 = jnp.float32
BF16 = jnp.bfloat16
VMEM = pl.BlockSpec(memory_space=pltpu.VMEM)
SMEM = pl.BlockSpec(memory_space=pltpu.SMEM)


def params(mib):
    return pltpu.CompilerParams(vmem_limit_bytes=mib * 2**20)


def dot(a, b, a_dim, b_dim):
    return lax.dot_general(a, b, (((a_dim,), (b_dim,)), ((), ())), preferred_element_type=F32)


def three_pieces(value):
    high = value.astype(BF16)
    rest = value - high.astype(F32)
    middle = rest.astype(BF16)
    low = (rest - middle.astype(F32)).astype(BF16)
    return high, middle, low


def pack_kernel(tok_hbm, grad_hbm, ids_hbm, weight_hbm, out_ref, ids_ref, weight_ref, sems):
    copies = [
        pltpu.make_async_copy(ids_hbm, ids_ref, sems.at[0]),
        pltpu.make_async_copy(weight_hbm, weight_ref, sems.at[1]),
        pltpu.make_async_copy(tok_hbm, out_ref.at[:, pl.ds(0, D)], sems.at[2]),
        pltpu.make_async_copy(grad_hbm, out_ref.at[:, pl.ds(D, D)], sems.at[3]),
    ]
    for copy in copies:
        copy.start()
    copies[0].wait()
    copies[1].wait()
    pieces = (ids_ref[...].astype(F32).astype(BF16),) + three_pieces(weight_ref[...])
    rows = lax.broadcasted_iota(jnp.int32, (TOP, META), 0)
    lanes = lax.broadcasted_iota(jnp.int32, (TOP, META), 1)
    meta = jnp.zeros((TOK, META), F32)
    for i, piece in enumerate(pieces):
        place = jnp.where(lanes == rows + i * TOP, 1.0, 0.0).astype(BF16)
        meta = meta + dot(piece, place, 0, 0)
    out_ref[:, 2 * D :] = meta.astype(BF16)
    copies[2].wait()
    copies[3].wait()


def pack(tokens, out_grad, ids_t, weight_t):
    return pl.pallas_call(
        pack_kernel,
        out_shape=jax.ShapeDtypeStruct((TOK, COLS), BF16),
        in_specs=[pl.BlockSpec(memory_space=pltpu.HBM)] * 4,
        out_specs=VMEM,
        scratch_shapes=[
            pltpu.VMEM((TOP, TOK), jnp.int32),
            pltpu.VMEM((TOP, TOK), F32),
            pltpu.SemaphoreType.DMA((4,)),
        ],
        compiler_params=params(4),
        name="pack_rows",
    )(tokens, out_grad, ids_t, weight_t)


def spread_kernel(first_ref, *refs):
    blocks, (send_ref, all_ref, mask_ref, weight_ref) = refs[:BLOCKS], refs[BLOCKS:]
    for j, block in enumerate(blocks[:-1]):
        all_ref[min(j, PLANES - 1) * TOK : min(j, PLANES - 1) * TOK + TOK, : block.shape[1]] = block[...]
    all_ref[GROUP - TOK :, D:] = blocks[-1][...]
    meta = all_ref[:, 2 * D :].astype(F32)
    shape = (GROUP, ROWS)
    lane = lax.broadcasted_iota(jnp.int32, shape, 1)
    row = lax.broadcasted_iota(jnp.int32, shape, 0)
    expert = (first_ref[0] + lane // (PLANES * SLOTS)).astype(F32)
    named = jnp.zeros(shape, F32)
    weight = jnp.zeros(shape, F32)
    for k in range(TOP):
        hit = meta[:, k : k + 1] == expert
        w = meta[:, TOP + k : TOP + k + 1] + meta[:, 2 * TOP + k : 2 * TOP + k + 1]
        w = w + meta[:, 3 * TOP + k : 3 * TOP + k + 1]
        named = jnp.where(hit, 1.0, named)
        weight = jnp.where(hit, w, weight)
    ri = lax.broadcasted_iota(jnp.int32, (GROUP, GROUP), 0)
    ci = lax.broadcasted_iota(jnp.int32, (GROUP, GROUP), 1)
    earlier = jnp.where((ri // TOK == ci // TOK) & (ci < ri), 1.0, 0.0).astype(BF16)
    slot = dot(earlier, named.astype(BF16), 1, 0)
    wanted = (lane % SLOTS).astype(F32)
    source = (lane // SLOTS) % PLANES
    mask = jnp.where((slot == wanted) & (source == row // TOK), named, 0.0)
    weight = weight * mask
    mask_ref[...] = mask.astype(BF16)
    weight_ref[...] = weight
    pick = mask.T.astype(BF16)
    scale = jnp.sum(weight.T, axis=1, keepdims=True)
    for i in range(0, D, 512):
        send_ref[:, i : i + 512] = dot(pick, all_ref[:, i : i + 512], 1, 0).astype(BF16)
    for i in range(D, 2 * D, 512):
        send_ref[:, i : i + 512] = (dot(pick, all_ref[:, i : i + 512], 1, 0) * scale).astype(BF16)


def spread(first, blocks):
    return pl.pallas_call(
        spread_kernel,
        out_shape=(
            jax.ShapeDtypeStruct((ROWS, 2 * D), BF16),
            jax.ShapeDtypeStruct((GROUP, COLS), BF16),
            jax.ShapeDtypeStruct((GROUP, ROWS), BF16),
            jax.ShapeDtypeStruct((GROUP, ROWS), F32),
        ),
        in_specs=[SMEM] + [VMEM] * BLOCKS,
        out_specs=(VMEM,) * 4,
        compiler_params=params(10),
        name="spread_rows",
    )(first, *blocks)


def expert_kernel(in_ref, gate_ref, up_ref, down_ref, back_ref, hidden_ref, pre_ref, up_pre_ref):
    w_gate = gate_ref[0]
    w_up = up_ref[0]
    w_down = down_ref[0]
    rows = in_ref[:, :D]
    gate = dot(rows, w_gate, 1, 0)
    up = dot(rows, w_up, 1, 0)
    sig = jax.nn.sigmoid(gate)
    act = gate * sig
    hidden = (act * up).astype(BF16)
    hidden_ref[...] = hidden
    hidden_grad = dot(in_ref[:, D:], w_down, 1, 1)
    pre = (hidden_grad * up * sig * (1.0 + gate * (1.0 - sig))).astype(BF16)
    up_pre = (hidden_grad * act).astype(BF16)
    pre_ref[...] = pre
    up_pre_ref[...] = up_pre
    for i in range(0, D, 512):
        back_ref[:, i : i + 512] = dot(hidden, down_ref[0, :, i : i + 512], 1, 0).astype(BF16)
    for i in range(0, D, 512):
        back_ref[:, D + i : D + i + 512] = (
            dot(pre, gate_ref[0, i : i + 512, :], 1, 1) + dot(up_pre, up_ref[0, i : i + 512, :], 1, 1)
        ).astype(BF16)


def expert(rows, gate_weight, up_weight, down_weight):
    act = jax.ShapeDtypeStruct((ROWS, HALF), BF16)
    return pl.pallas_call(
        expert_kernel,
        out_shape=(jax.ShapeDtypeStruct((ROWS, 2 * D), BF16), act, act, act),
        in_specs=[VMEM] * 4,
        out_specs=(VMEM,) * 4,
        compiler_params=params(16),
        cost_estimate=pl.CostEstimate(
            flops=12 * ROWS * D * HALF, bytes_accessed=8 * 2**20, transcendentals=ROWS * HALF
        ),
        name="expert_rows",
    )(rows, gate_weight, up_weight, down_weight)


def weight_grad_kernel(x_a, g_a, x_b, g_b, h_a, p_a, u_a, h_b, p_b, u_b, gate_ref, up_ref, down_ref):
    gate_ref[0] = (dot(x_a[...], p_a[...], 0, 0) + dot(x_b[...], p_b[...], 0, 0)).astype(BF16)
    up_ref[0] = (dot(x_a[...], u_a[...], 0, 0) + dot(x_b[...], u_b[...], 0, 0)).astype(BF16)
    down_ref[0] = (dot(h_a[...], g_a[...], 0, 0) + dot(h_b[...], g_b[...], 0, 0)).astype(BF16)


def weight_grads(own, other, own_acts, other_acts):
    width = 512
    steps = D // width
    x_spec = pl.BlockSpec((ROWS, width), lambda i: (0, i))
    g_spec = pl.BlockSpec((ROWS, width), lambda i: (0, i + steps))
    act_spec = pl.BlockSpec((ROWS, HALF), lambda i: (0, 0))
    wide = pl.BlockSpec((1, width, HALF), lambda i: (0, i, 0))
    return pl.pallas_call(
        weight_grad_kernel,
        grid=(steps,),
        out_shape=(
            jax.ShapeDtypeStruct((1, D, HALF), BF16),
            jax.ShapeDtypeStruct((1, D, HALF), BF16),
            jax.ShapeDtypeStruct((1, HALF, D), BF16),
        ),
        in_specs=[x_spec, g_spec, x_spec, g_spec] + [act_spec] * 6,
        out_specs=(wide, wide, pl.BlockSpec((1, HALF, width), lambda i: (0, 0, i))),
        compiler_params=params(20),
        cost_estimate=pl.CostEstimate(
            flops=12 * ROWS * D * HALF, bytes_accessed=12 * 2**20, transcendentals=0
        ),
        name="weight_grads",
    )(own, own, other, other, *own_acts, *other_acts)


def combine_kernel(first_ref, back_ref, all_ref, mask_ref, weight_ref, *out_refs):
    def put(value, begin):
        value = value.astype(BF16)
        end = begin + value.shape[1]
        for j in range(PLANES - 1):
            out_refs[j][:, begin:end] = value[j * TOK : (j + 1) * TOK]
        if begin < D:
            out_refs[PLANES - 1][:, begin:end] = value[GROUP - TOK :]
        else:
            out_refs[PLANES][:, begin - D : end - D] = value[GROUP - TOK :]

    mask = mask_ref[...]
    weight = weight_ref[...]
    high = weight.astype(BF16)
    low = (weight - high.astype(F32)).astype(BF16)
    products = jnp.zeros((GROUP, ROWS), F32)
    for i in range(0, D, 512):
        part = back_ref[:, i : i + 512]
        put(dot(high, part, 1, 0) + dot(low, part, 1, 0), i)
        products = products + dot(all_ref[:, D + i : D + i + 512], part, 1, 1)
    for i in range(D, 2 * D, 512):
        put(dot(mask, back_ref[:, i : i + 512], 1, 0), i)
    meta = all_ref[:, 2 * D :].astype(F32)
    products = products * mask.astype(F32)
    lane = lax.broadcasted_iota(jnp.int32, (GROUP, ROWS), 1)
    expert_of = (first_ref[0] + lane // (PLANES * SLOTS)).astype(F32)
    place = lax.broadcasted_iota(jnp.int32, (GROUP, META), 1)
    tail = jnp.zeros((GROUP, META), F32)
    for k in range(TOP):
        hit = meta[:, k : k + 1] == expert_of
        value = jnp.sum(jnp.where(hit, products, 0.0), axis=1, keepdims=True)
        for i, piece in enumerate(three_pieces(value)):
            tail = jnp.where(place == i * TOP + k, piece.astype(F32), tail)
    put(tail, 2 * D)


def combine(first, back, gathered, mask, weight):
    block = jax.ShapeDtypeStruct((TOK, COLS), BF16)
    halves = (jax.ShapeDtypeStruct((TOK, D), BF16), jax.ShapeDtypeStruct((TOK, COLS - D), BF16))
    return pl.pallas_call(
        combine_kernel,
        out_shape=(block,) * (PLANES - 1) + halves,
        in_specs=[SMEM] + [VMEM] * 4,
        out_specs=(VMEM,) * BLOCKS,
        compiler_params=params(10),
        name="combine_rows",
    )(first, back, gathered, mask, weight)


def relay_kernel(mine_up, next_up, first_half, mine_down, next_down, second_half, up_ref, down_ref):
    up = mine_up[...].astype(F32) + next_up[...].astype(F32)
    up_ref[:, D:] = up[:, D:].astype(BF16)
    up_ref[:, :D] = (up[:, :D] + first_half[...].astype(F32)).astype(BF16)
    down = mine_down[...].astype(F32) + next_down[...].astype(F32)
    down_ref[:, :D] = down[:, :D].astype(BF16)
    down_ref[:, D:] = (down[:, D:] + second_half[...].astype(F32)).astype(BF16)


def relay(*parts):
    block = jax.ShapeDtypeStruct((TOK, COLS), BF16)
    return pl.pallas_call(
        relay_kernel,
        out_shape=(block, block),
        in_specs=[VMEM] * 6,
        out_specs=(VMEM, VMEM),
        compiler_params=params(4),
        name="relay_rows",
    )(*parts)


def total_kernel(*refs):
    *in_refs, out_ref, grad_ref, route_ref = refs
    total = in_refs[0][...].astype(F32)
    for ref in in_refs[1:]:
        total = total + ref[...].astype(F32)
    out_ref[...] = total[:, :D].astype(BF16)
    grad_ref[...] = total[:, D : 2 * D].astype(BF16)
    tail = total[:, 2 * D :].T
    route_ref[...] = tail[:TOP] + tail[TOP : 2 * TOP] + tail[2 * TOP : 3 * TOP]


def totals(*parts):
    return pl.pallas_call(
        total_kernel,
        out_shape=(
            jax.ShapeDtypeStruct((TOK, D), BF16),
            jax.ShapeDtypeStruct((TOK, D), BF16),
            jax.ShapeDtypeStruct((TOP, TOK), F32),
        ),
        in_specs=[VMEM] * len(parts),
        out_specs=(VMEM, VMEM, VMEM),
        compiler_params=params(4),
        name="total_rows",
    )(*parts)


def swap_cores(value):
    return lax.ppermute(value, "core", [(0, 1), (1, 0)])


def over_plane(value):
    blocks = value.reshape(CHIPS, PLANES * SLOTS, 2 * D)
    return lax.all_to_all(blocks, ("y", "x"), 0, 0, tiled=True).reshape(ROWS, 2 * D)


def shift(value, step):
    return lax.ppermute(value, "z", [(i, (i + step) % PLANES) for i in range(PLANES)])


def spread_z(own):
    below, above = shift(own, 1), shift(own, -1)
    below2, above2 = shift(own, 2), shift(own, -2)
    half, other_half = shift(below2[:, :D], 2), shift(above2[:, D:], -2)
    below3, above3 = shift(below2, 1), shift(above2, -1)
    return own, below, above, below2, above2, below3, above3, half, other_half


def reduce_z(blocks):
    own, below, above, below2, above2, below3, above3, half, other_half = blocks
    up = (above2, shift(above3, 1), shift(half, 2))
    down = (below2, shift(below3, -1), shift(other_half, -2))
    near = (shift(above, 1), shift(below, -1))
    up, down = relay(*up, *down)
    return totals(own, *near, shift(up, 2), shift(down, -2))


def body(tokens, expert_ids, route_weight, out_grad, gate_weight, up_weight, down_weight):
    first = (lax.axis_index("z") * CHIPS).astype(jnp.int32).reshape(1)
    blocks = spread_z(pack(tokens, out_grad, expert_ids.T, route_weight.T))
    send, gathered, mask, weight = spread(first, blocks)
    own = over_plane(send)
    other = swap_cores(own)
    own_back, *own_acts = expert(own, gate_weight, up_weight, down_weight)
    other_back, *other_acts = expert(other, gate_weight, up_weight, down_weight)
    from_other = swap_cores(other_back)
    summed = (own_back.astype(F32) + from_other.astype(F32)).astype(BF16)
    back = over_plane(summed)
    gate_grad, up_grad, down_grad = weight_grads(own, other, own_acts, other_acts)
    layer_out, token_grad, route_t = reduce_z(combine(first, back, gathered, mask, weight))
    return layer_out, token_grad, route_t.T, gate_grad, up_grad, down_grad


def solution(mesh):
    fine = Mesh(mesh.devices.reshape(SIZES), AXES)
    rows, pieces = P(AXES, None), P(AXES, None, None)
    return jax.shard_map(
        body,
        mesh=fine,
        in_specs=(rows, rows, rows, rows, pieces, pieces, pieces),
        out_specs=(rows, rows, rows, pieces, pieces, pieces),
        check_vma=False,
    )
```

```python
import functools

import jax
import jax.numpy as jnp
from jax import lax
from jax.experimental import pallas as pl
from jax.experimental.pallas import tpu as pltpu
from jax.sharding import Mesh, PartitionSpec as P

AXES = ("z", "y", "x", "core")
SIZES = (8, 4, 4, 2)
PLANES = 8
CHIPS = 16
TOK = 16
TOP = 8
SLOTS = 2
D = 2048
HALF = 384
META = 128
COLS = 2 * D + META
GROUP = PLANES * TOK
SENT = PLANES * SLOTS
ROWS = CHIPS * SENT
BLOCKS = PLANES + 1
F32 = jnp.float32
BF16 = jnp.bfloat16
VMEM = pl.BlockSpec(memory_space=pltpu.VMEM)
SMEM = pl.BlockSpec(memory_space=pltpu.SMEM)


def params(mib):
    return pltpu.CompilerParams(vmem_limit_bytes=mib * 2**20)


def dot(a, b, a_dim, b_dim):
    return lax.dot_general(a, b, (((a_dim,), (b_dim,)), ((), ())), preferred_element_type=F32)


def three_pieces(value):
    high = value.astype(BF16)
    rest = value - high.astype(F32)
    middle = rest.astype(BF16)
    low = (rest - middle.astype(F32)).astype(BF16)
    return high, middle, low


def pack_kernel(tok_hbm, grad_hbm, ids_hbm, weight_hbm, out_ref, ids_ref, weight_ref, sems):
    copies = [
        pltpu.make_async_copy(ids_hbm, ids_ref, sems.at[0]),
        pltpu.make_async_copy(weight_hbm, weight_ref, sems.at[1]),
        pltpu.make_async_copy(tok_hbm, out_ref.at[:, pl.ds(0, D)], sems.at[2]),
        pltpu.make_async_copy(grad_hbm, out_ref.at[:, pl.ds(D, D)], sems.at[3]),
    ]
    for copy in copies:
        copy.start()
    copies[0].wait()
    copies[1].wait()
    pieces = (ids_ref[...].astype(F32).astype(BF16),) + three_pieces(weight_ref[...])
    rows = lax.broadcasted_iota(jnp.int32, (TOP, META), 0)
    lanes = lax.broadcasted_iota(jnp.int32, (TOP, META), 1)
    meta = jnp.zeros((TOK, META), F32)
    for i, piece in enumerate(pieces):
        place = jnp.where(lanes == rows + i * TOP, 1.0, 0.0).astype(BF16)
        meta = meta + dot(piece, place, 0, 0)
    out_ref[:, 2 * D :] = meta.astype(BF16)
    copies[2].wait()
    copies[3].wait()


def pack(tokens, out_grad, ids_t, weight_t):
    return pl.pallas_call(
        pack_kernel,
        out_shape=jax.ShapeDtypeStruct((TOK, COLS), BF16),
        in_specs=[pl.BlockSpec(memory_space=pltpu.HBM)] * 4,
        out_specs=VMEM,
        scratch_shapes=[
            pltpu.VMEM((TOP, TOK), jnp.int32),
            pltpu.VMEM((TOP, TOK), F32),
            pltpu.SemaphoreType.DMA((4,)),
        ],
        compiler_params=params(63),
        name="pack_rows",
    )(tokens, out_grad, ids_t, weight_t)


def spread_kernel(first_ref, *refs):
    blocks, (send_ref, all_ref, mask_ref, weight_ref) = refs[:BLOCKS], refs[BLOCKS:]
    for j, block in enumerate(blocks[:-1]):
        all_ref[min(j, PLANES - 1) * TOK : min(j, PLANES - 1) * TOK + TOK, : block.shape[1]] = block[...]
    all_ref[GROUP - TOK :, D:] = blocks[-1][...]
    meta = all_ref[:, 2 * D :].astype(F32)
    shape = (GROUP, ROWS)
    lane = lax.broadcasted_iota(jnp.int32, shape, 1)
    row = lax.broadcasted_iota(jnp.int32, shape, 0)
    expert = (first_ref[0] + lane // (PLANES * SLOTS)).astype(F32)
    named = jnp.zeros(shape, F32)
    weight = jnp.zeros(shape, F32)
    for k in range(TOP):
        hit = meta[:, k : k + 1] == expert
        w = meta[:, TOP + k : TOP + k + 1] + meta[:, 2 * TOP + k : 2 * TOP + k + 1]
        w = w + meta[:, 3 * TOP + k : 3 * TOP + k + 1]
        named = jnp.where(hit, 1.0, named)
        weight = jnp.where(hit, w, weight)
    ri = lax.broadcasted_iota(jnp.int32, (GROUP, GROUP), 0)
    ci = lax.broadcasted_iota(jnp.int32, (GROUP, GROUP), 1)
    earlier = jnp.where((ri // TOK == ci // TOK) & (ci < ri), 1.0, 0.0).astype(BF16)
    slot = dot(earlier, named.astype(BF16), 1, 0)
    wanted = (lane % SLOTS).astype(F32)
    source = (lane // SLOTS) % PLANES
    mask = jnp.where((slot == wanted) & (source == row // TOK), named, 0.0)
    weight = weight * mask
    mask_ref[...] = mask.astype(BF16)
    weight_ref[...] = weight
    pick = mask.T.astype(BF16)
    scale = jnp.sum(weight.T, axis=1, keepdims=True)
    for i in range(0, D, 512):
        picked = dot(pick, all_ref[:, i : i + 512], 1, 0)
        send_ref[:, :SENT, i : i + 512] = picked.astype(BF16).reshape(CHIPS, SENT, 512)
        picked = dot(pick, all_ref[:, D + i : D + i + 512], 1, 0) * scale
        send_ref[:, SENT:, i : i + 512] = picked.astype(BF16).reshape(CHIPS, SENT, 512)


def spread(first, blocks):
    return pl.pallas_call(
        spread_kernel,
        out_shape=(
            jax.ShapeDtypeStruct((CHIPS, 2 * SENT, D), BF16),
            jax.ShapeDtypeStruct((GROUP, COLS), BF16),
            jax.ShapeDtypeStruct((GROUP, ROWS), BF16),
            jax.ShapeDtypeStruct((GROUP, ROWS), F32),
        ),
        in_specs=[SMEM] + [VMEM] * BLOCKS,
        out_specs=(VMEM,) * 4,
        compiler_params=params(10),
        name="spread_rows",
    )(first, *blocks)


def forward_kernel(in_ref, gate_ref, up_ref, down_ref, back_ref, hidden_ref, gate_out, up_out):
    rows = in_ref[...]
    gate = dot(rows, gate_ref[0], 1, 0)
    up = dot(rows, up_ref[0], 1, 0)
    gate_out[...] = gate
    up_out[...] = up
    hidden = (gate * jax.nn.sigmoid(gate) * up).astype(BF16)
    hidden_ref[...] = hidden
    for i in range(0, D, 512):
        back_ref[:, i : i + 512] = dot(hidden, down_ref[0, :, i : i + 512], 1, 0).astype(BF16)


def backward_kernel(in_ref, gate_in, up_in, gate_ref, up_ref, down_ref, back_ref, pre_ref, up_pre_ref):
    gate = gate_in[...]
    sig = jax.nn.sigmoid(gate)
    hidden_grad = dot(in_ref[...], down_ref[0], 1, 1)
    pre = (hidden_grad * up_in[...] * sig * (1.0 + gate * (1.0 - sig))).astype(BF16)
    up_pre = (hidden_grad * gate * sig).astype(BF16)
    pre_ref[...] = pre
    up_pre_ref[...] = up_pre
    for i in range(0, D, 512):
        back_ref[:, i : i + 512] = (
            dot(pre, gate_ref[0, i : i + 512, :], 1, 1) + dot(up_pre, up_ref[0, i : i + 512, :], 1, 1)
        ).astype(BF16)


COST = pl.CostEstimate(flops=6 * ROWS * D * HALF, bytes_accessed=5 * 2**20, transcendentals=ROWS * HALF)
WIDE = jax.ShapeDtypeStruct((ROWS, D), BF16)
ACT = jax.ShapeDtypeStruct((ROWS, HALF), BF16)
ACT32 = jax.ShapeDtypeStruct((ROWS, HALF), F32)


def forward(rows, weights):
    return pl.pallas_call(
        forward_kernel,
        out_shape=(WIDE, ACT, ACT32, ACT32),
        in_specs=[VMEM] * 4,
        out_specs=(VMEM,) * 4,
        compiler_params=params(16),
        cost_estimate=COST,
        name="forward_rows",
    )(rows, *weights)


def backward(rows, gate, up, weights):
    return pl.pallas_call(
        backward_kernel,
        out_shape=(WIDE, ACT, ACT),
        in_specs=[VMEM] * 6,
        out_specs=(VMEM,) * 3,
        compiler_params=params(16),
        cost_estimate=COST,
        name="backward_rows",
    )(rows, gate, up, *weights)


def pair_sum_kernel(out_a, out_b, grad_a, grad_b, sum_ref):
    for begin, a_ref, b_ref in ((0, out_a, out_b), (SENT, grad_a, grad_b)):
        total = a_ref[...].astype(F32) + b_ref[...].astype(F32)
        sum_ref[:, begin : begin + SENT, :] = total.astype(BF16).reshape(CHIPS, SENT, D)


def pair_sum(*parts):
    return pl.pallas_call(
        pair_sum_kernel,
        out_shape=jax.ShapeDtypeStruct((CHIPS, 2 * SENT, D), BF16),
        in_specs=[VMEM] * 4,
        out_specs=VMEM,
        compiler_params=params(12),
        name="sum_halves",
    )(*parts)


def weight_grad_kernel(x_a, g_a, x_b, g_b, h_a, p_a, u_a, h_b, p_b, u_b, gate_ref, up_ref, down_ref):
    gate_ref[0] = (dot(x_a[...], p_a[...], 0, 0) + dot(x_b[...], p_b[...], 0, 0)).astype(BF16)
    up_ref[0] = (dot(x_a[...], u_a[...], 0, 0) + dot(x_b[...], u_b[...], 0, 0)).astype(BF16)
    down_ref[0] = (dot(h_a[...], g_a[...], 0, 0) + dot(h_b[...], g_b[...], 0, 0)).astype(BF16)


def weight_grads(own_rows, own_grads, other_rows, other_grads, own_acts, other_acts):
    width = 512
    steps = D // width
    x_spec = pl.BlockSpec((ROWS, width), lambda i: (0, i))
    act_spec = pl.BlockSpec((ROWS, HALF), lambda i: (0, 0))
    wide = pl.BlockSpec((1, width, HALF), lambda i: (0, i, 0))
    return pl.pallas_call(
        weight_grad_kernel,
        grid=(steps,),
        out_shape=(
            jax.ShapeDtypeStruct((1, D, HALF), BF16),
            jax.ShapeDtypeStruct((1, D, HALF), BF16),
            jax.ShapeDtypeStruct((1, HALF, D), BF16),
        ),
        in_specs=[x_spec] * 4 + [act_spec] * 6,
        out_specs=(wide, wide, pl.BlockSpec((1, HALF, width), lambda i: (0, 0, i))),
        compiler_params=params(20),
        cost_estimate=pl.CostEstimate(
            flops=12 * ROWS * D * HALF, bytes_accessed=12 * 2**20, transcendentals=0
        ),
        name="weight_grads",
    )(own_rows, own_grads, other_rows, other_grads, *own_acts, *other_acts)


def combine_kernel(first_ref, back_ref, all_ref, mask_ref, weight_ref, *out_refs):
    own, below2, above2, down_pair, up_pair, half, other_half = out_refs
    places = ((own, 0), (down_pair, TOK), (up_pair, TOK), (below2, 0), (above2, 0), (down_pair, 0), (up_pair, 0))

    def put(value, begin):
        value = value.astype(BF16)
        end = begin + value.shape[1]
        for j, (ref, row) in enumerate(places):
            ref[row : row + TOK, begin:end] = value[j * TOK : (j + 1) * TOK]
        if begin < D:
            half[:, begin:end] = value[GROUP - TOK :]
        else:
            other_half[:, begin - D : end - D] = value[GROUP - TOK :]

    mask = mask_ref[...]
    weight = weight_ref[...]
    high = weight.astype(BF16)
    low = (weight - high.astype(F32)).astype(BF16)
    products = jnp.zeros((GROUP, ROWS), F32)
    for i in range(0, D, 512):
        part = back_ref[:, :SENT, i : i + 512].reshape(ROWS, 512)
        put(dot(high, part, 1, 0) + dot(low, part, 1, 0), i)
        products = products + dot(all_ref[:, D + i : D + i + 512], part, 1, 1)
        put(dot(mask, back_ref[:, SENT:, i : i + 512].reshape(ROWS, 512), 1, 0), D + i)
    meta = all_ref[:, 2 * D :].astype(F32)
    products = products * mask.astype(F32)
    lane = lax.broadcasted_iota(jnp.int32, (GROUP, ROWS), 1)
    expert_of = (first_ref[0] + lane // (PLANES * SLOTS)).astype(F32)
    place = lax.broadcasted_iota(jnp.int32, (GROUP, META), 1)
    tail = jnp.zeros((GROUP, META), F32)
    for k in range(TOP):
        hit = meta[:, k : k + 1] == expert_of
        value = jnp.sum(jnp.where(hit, products, 0.0), axis=1, keepdims=True)
        for i, piece in enumerate(three_pieces(value)):
            tail = jnp.where(place == i * TOP + k, piece.astype(F32), tail)
    put(tail, 2 * D)


def combine(first, back, gathered, mask, weight):
    block = jax.ShapeDtypeStruct((TOK, COLS), BF16)
    pair = jax.ShapeDtypeStruct((2 * TOK, COLS), BF16)
    halves = (jax.ShapeDtypeStruct((TOK, D), BF16), jax.ShapeDtypeStruct((TOK, COLS - D), BF16))
    return pl.pallas_call(
        combine_kernel,
        out_shape=(block, block, block, pair, pair) + halves,
        in_specs=[SMEM] + [VMEM] * 4,
        out_specs=(VMEM,) * 7,
        compiler_params=params(10),
        name="combine_rows",
    )(first, back, gathered, mask, weight)


def relay_kernel(mine_up, next_up, first_half, mine_down, next_down, second_half, up_ref, down_ref):
    up = mine_up[...].astype(F32) + next_up[:TOK].astype(F32)
    up_ref[:, D:] = up[:, D:].astype(BF16)
    up_ref[:, :D] = (up[:, :D] + first_half[...].astype(F32)).astype(BF16)
    down = mine_down[...].astype(F32) + next_down[:TOK].astype(F32)
    down_ref[:, :D] = down[:, :D].astype(BF16)
    down_ref[:, D:] = (down[:, D:] + second_half[...].astype(F32)).astype(BF16)


def relay(*parts):
    block = jax.ShapeDtypeStruct((TOK, COLS), BF16)
    return pl.pallas_call(
        relay_kernel,
        out_shape=(block, block),
        in_specs=[VMEM] * 6,
        out_specs=(VMEM, VMEM),
        compiler_params=params(4),
        name="relay_rows",
    )(*parts)


def total_kernel(*refs):
    *in_refs, out_ref, grad_ref, route_ref = refs
    total = in_refs[0][...].astype(F32)
    for ref in in_refs[1:]:
        total = total + ref[ref.shape[0] - TOK :].astype(F32)
    out_ref[...] = total[:, :D].astype(BF16)
    grad_ref[...] = total[:, D : 2 * D].astype(BF16)
    tail = total[:, 2 * D :].T
    route_ref[...] = tail[:TOP] + tail[TOP : 2 * TOP] + tail[2 * TOP : 3 * TOP]


def totals(*parts):
    return pl.pallas_call(
        total_kernel,
        out_shape=(
            jax.ShapeDtypeStruct((TOK, D), BF16),
            jax.ShapeDtypeStruct((TOK, D), BF16),
            jax.ShapeDtypeStruct((TOP, TOK), F32),
        ),
        in_specs=[VMEM] * len(parts),
        out_specs=(VMEM, VMEM, VMEM),
        compiler_params=params(4),
        name="total_rows",
    )(*parts)


def swap_cores(value):
    return lax.ppermute(value, "core", [(0, 1), (1, 0)])


def over_plane(blocks):
    return lax.all_to_all(blocks, ("y", "x"), 0, 0, tiled=True)


def shift(value, step):
    return lax.ppermute(value, "z", [(i, (i + step) % PLANES) for i in range(PLANES)])


def spread_z(own):
    below, above = shift(own, 1), shift(own, -1)
    below2, above2 = shift(own, 2), shift(own, -2)
    half, other_half = shift(below2[:, :D], 2), shift(above2[:, D:], -2)
    below3, above3 = shift(below2, 1), shift(above2, -1)
    return own, below, above, below2, above2, below3, above3, half, other_half


def reduce_z(own, below2, above2, down_pair, up_pair, half, other_half):
    from_above, from_below = shift(down_pair, -1), shift(up_pair, 1)
    up, down = relay(above2, from_below, shift(half, 2), below2, from_above, shift(other_half, -2))
    return totals(own, from_above, from_below, shift(up, 2), shift(down, -2))


def body(tokens, expert_ids, route_weight, out_grad, gate_weight, up_weight, down_weight):
    first = (lax.axis_index("z") * CHIPS).astype(jnp.int32).reshape(1)
    weights = (gate_weight, up_weight, down_weight)
    blocks = spread_z(pack(tokens, out_grad, expert_ids.T, route_weight.T))
    send, gathered, mask, weight = spread(first, blocks)
    arrived = over_plane(send)
    rows = arrived[:, :SENT].reshape(ROWS, D)
    grads = arrived[:, SENT:].reshape(ROWS, D)
    other_rows, other_grads = swap_cores(rows), swap_cores(grads)
    out_a, hidden_a, gate_a, up_a = forward(rows, weights)
    hidden_a, other_rows = lax.optimization_barrier((hidden_a, other_rows))
    out_b, hidden_b, gate_b, up_b = forward(other_rows, weights)
    grad_b, pre_b, up_pre_b = backward(other_grads, gate_b, up_b, weights)
    grad_a, pre_a, up_pre_a = backward(grads, gate_a, up_a, weights)
    summed = pair_sum(out_a, swap_cores(out_b), grad_a, swap_cores(grad_b))
    back = over_plane(summed)
    gate_grad, up_grad, down_grad = weight_grads(
        rows, grads, other_rows, other_grads, (hidden_a, pre_a, up_pre_a), (hidden_b, pre_b, up_pre_b)
    )
    layer_out, token_grad, route_t = reduce_z(*combine(first, back, gathered, mask, weight))
    return layer_out, token_grad, route_t.T, gate_grad, up_grad, down_grad


def solution(mesh):
    fine = Mesh(mesh.devices.reshape(SIZES), AXES)
    rows, pieces = P(AXES, None), P(AXES, None, None)
    return jax.shard_map(
        body,
        mesh=fine,
        in_specs=(rows, rows, rows, rows, pieces, pieces, pieces),
        out_specs=(rows, rows, rows, pieces, pieces, pieces),
        check_vma=False,
    )
```

```python
import functools

import jax
import jax.numpy as jnp
from jax import lax
from jax.experimental import pallas as pl
from jax.experimental.pallas import tpu as pltpu
from jax.sharding import Mesh, PartitionSpec as P

AXES = ("z", "y", "x", "core")
SIZES = (8, 4, 4, 2)
PLANES = 8
CHIPS = 16
TOK = 16
TOP = 8
SLOTS = 2
D = 2048
HALF = 384
META = 128
COLS = 2 * D + META
GROUP = PLANES * TOK
SENT = PLANES * SLOTS
ROWS = CHIPS * SENT
BLOCKS = PLANES + 1
F32 = jnp.float32
BF16 = jnp.bfloat16
VMEM = pl.BlockSpec(memory_space=pltpu.VMEM)
SMEM = pl.BlockSpec(memory_space=pltpu.SMEM)


def params(mib):
    return pltpu.CompilerParams(vmem_limit_bytes=mib * 2**20)


def dot(a, b, a_dim, b_dim):
    return lax.dot_general(a, b, (((a_dim,), (b_dim,)), ((), ())), preferred_element_type=F32)


def three_pieces(value):
    high = value.astype(BF16)
    rest = value - high.astype(F32)
    middle = rest.astype(BF16)
    low = (rest - middle.astype(F32)).astype(BF16)
    return high, middle, low


def pack_kernel(tok_hbm, grad_hbm, ids_hbm, weight_hbm, out_ref, ids_ref, weight_ref, sems):
    copies = [
        pltpu.make_async_copy(ids_hbm, ids_ref, sems.at[0]),
        pltpu.make_async_copy(weight_hbm, weight_ref, sems.at[1]),
        pltpu.make_async_copy(tok_hbm, out_ref.at[:, pl.ds(0, D)], sems.at[2]),
        pltpu.make_async_copy(grad_hbm, out_ref.at[:, pl.ds(D, D)], sems.at[3]),
    ]
    for copy in copies:
        copy.start()
    copies[0].wait()
    copies[1].wait()
    pieces = (ids_ref[...].astype(F32).astype(BF16),) + three_pieces(weight_ref[...])
    rows = lax.broadcasted_iota(jnp.int32, (TOP, META), 0)
    lanes = lax.broadcasted_iota(jnp.int32, (TOP, META), 1)
    meta = jnp.zeros((TOK, META), F32)
    for i, piece in enumerate(pieces):
        place = jnp.where(lanes == rows + i * TOP, 1.0, 0.0).astype(BF16)
        meta = meta + dot(piece, place, 0, 0)
    out_ref[:, 2 * D :] = meta.astype(BF16)
    copies[2].wait()
    copies[3].wait()


def pack(tokens, out_grad, ids_t, weight_t):
    return pl.pallas_call(
        pack_kernel,
        out_shape=jax.ShapeDtypeStruct((TOK, COLS), BF16),
        in_specs=[pl.BlockSpec(memory_space=pltpu.HBM)] * 4,
        out_specs=VMEM,
        scratch_shapes=[
            pltpu.VMEM((TOP, TOK), jnp.int32),
            pltpu.VMEM((TOP, TOK), F32),
            pltpu.SemaphoreType.DMA((4,)),
        ],
        compiler_params=params(63),
        name="pack_rows",
    )(tokens, out_grad, ids_t, weight_t)


def hold_kernel(gate_hbm, up_hbm, down_hbm, both_ref, down_ref, sems):
    copies = [
        pltpu.make_async_copy(gate_hbm.at[0], both_ref.at[:, pl.ds(0, HALF)], sems.at[0]),
        pltpu.make_async_copy(up_hbm.at[0], both_ref.at[:, pl.ds(HALF, HALF)], sems.at[1]),
        pltpu.make_async_copy(down_hbm, down_ref, sems.at[2]),
    ]
    for copy in copies:
        copy.start()
    for copy in copies:
        copy.wait()


def hold(gate_weight, up_weight, down_weight):
    return pl.pallas_call(
        hold_kernel,
        out_shape=(jax.ShapeDtypeStruct((D, 2 * HALF), BF16), jax.ShapeDtypeStruct((1, HALF, D), BF16)),
        in_specs=[pl.BlockSpec(memory_space=pltpu.HBM)] * 3,
        out_specs=(VMEM, VMEM),
        scratch_shapes=[pltpu.SemaphoreType.DMA((3,))],
        compiler_params=params(16),
        name="hold_weights",
    )(gate_weight, up_weight, down_weight)


def spread_kernel(first_ref, *refs):
    blocks, (send_ref, all_ref, mask_ref, weight_ref) = refs[:BLOCKS], refs[BLOCKS:]
    for j, block in enumerate(blocks[:-1]):
        all_ref[min(j, PLANES - 1) * TOK : min(j, PLANES - 1) * TOK + TOK, : block.shape[1]] = block[...]
    all_ref[GROUP - TOK :, D:] = blocks[-1][...]
    meta = all_ref[:, 2 * D :].astype(F32)
    shape = (GROUP, ROWS)
    lane = lax.broadcasted_iota(jnp.int32, shape, 1)
    row = lax.broadcasted_iota(jnp.int32, shape, 0)
    expert = (first_ref[0] + lane // (PLANES * SLOTS)).astype(F32)
    named = jnp.zeros(shape, F32)
    weight = jnp.zeros(shape, F32)
    for k in range(TOP):
        hit = meta[:, k : k + 1] == expert
        w = meta[:, TOP + k : TOP + k + 1] + meta[:, 2 * TOP + k : 2 * TOP + k + 1]
        w = w + meta[:, 3 * TOP + k : 3 * TOP + k + 1]
        named = jnp.where(hit, 1.0, named)
        weight = jnp.where(hit, w, weight)
    ri = lax.broadcasted_iota(jnp.int32, (GROUP, GROUP), 0)
    ci = lax.broadcasted_iota(jnp.int32, (GROUP, GROUP), 1)
    earlier = jnp.where((ri // TOK == ci // TOK) & (ci < ri), 1.0, 0.0).astype(BF16)
    slot = dot(earlier, named.astype(BF16), 1, 0)
    wanted = (lane % SLOTS).astype(F32)
    source = (lane // SLOTS) % PLANES
    mask = jnp.where((slot == wanted) & (source == row // TOK), named, 0.0)
    weight = weight * mask
    mask_ref[...] = mask.astype(BF16)
    weight_ref[...] = weight
    pick = mask.T.astype(BF16)
    scale = jnp.sum(weight.T, axis=1, keepdims=True)
    for i in range(0, D, 512):
        picked = dot(pick, all_ref[:, i : i + 512], 1, 0)
        send_ref[:, :SENT, i : i + 512] = picked.astype(BF16).reshape(CHIPS, SENT, 512)
        picked = dot(pick, all_ref[:, D + i : D + i + 512], 1, 0) * scale
        send_ref[:, SENT:, i : i + 512] = picked.astype(BF16).reshape(CHIPS, SENT, 512)


def spread(first, blocks):
    return pl.pallas_call(
        spread_kernel,
        out_shape=(
            jax.ShapeDtypeStruct((CHIPS, 2 * SENT, D), BF16),
            jax.ShapeDtypeStruct((GROUP, COLS), BF16),
            jax.ShapeDtypeStruct((GROUP, ROWS), BF16),
            jax.ShapeDtypeStruct((GROUP, ROWS), F32),
        ),
        in_specs=[SMEM] + [VMEM] * BLOCKS,
        out_specs=(VMEM,) * 4,
        compiler_params=params(10),
        name="spread_rows",
    )(first, *blocks)


def forward_kernel(in_ref, both_ref, down_ref, back_ref, hidden_ref, gate_out, up_out):
    rows = in_ref[...]
    gate = dot(rows, both_ref[:, :HALF], 1, 0)
    up = dot(rows, both_ref[:, HALF:], 1, 0)
    gate_out[...] = gate
    up_out[...] = up
    hidden = (gate * jax.nn.sigmoid(gate) * up).astype(BF16)
    hidden_ref[...] = hidden
    for i in range(0, D, 512):
        back_ref[:, i : i + 512] = dot(hidden, down_ref[0, :, i : i + 512], 1, 0).astype(BF16)


def backward_kernel(in_ref, gate_in, up_in, both_ref, down_ref, back_ref, pre_ref):
    gate = gate_in[...]
    sig = jax.nn.sigmoid(gate)
    hidden_grad = dot(in_ref[...], down_ref[0], 1, 1)
    pre_ref[:, :HALF] = (hidden_grad * up_in[...] * sig * (1.0 + gate * (1.0 - sig))).astype(BF16)
    pre_ref[:, HALF:] = (hidden_grad * gate * sig).astype(BF16)
    for i in range(0, D, 512):
        back_ref[:, i : i + 512] = dot(pre_ref[...], both_ref[i : i + 512, :], 1, 1).astype(BF16)


COST = pl.CostEstimate(flops=6 * ROWS * D * HALF, bytes_accessed=5 * 2**20, transcendentals=ROWS * HALF)
WIDE = jax.ShapeDtypeStruct((ROWS, D), BF16)
ACT = jax.ShapeDtypeStruct((ROWS, HALF), BF16)
ACT32 = jax.ShapeDtypeStruct((ROWS, HALF), F32)


def forward(rows, weights):
    return pl.pallas_call(
        forward_kernel,
        out_shape=(WIDE, ACT, ACT32, ACT32),
        in_specs=[VMEM] * 3,
        out_specs=(VMEM,) * 4,
        compiler_params=params(16),
        cost_estimate=COST,
        name="forward_rows",
    )(rows, *weights)


def backward(rows, gate, up, weights):
    return pl.pallas_call(
        backward_kernel,
        out_shape=(WIDE, jax.ShapeDtypeStruct((ROWS, 2 * HALF), BF16)),
        in_specs=[VMEM] * 5,
        out_specs=(VMEM,) * 2,
        compiler_params=params(16),
        cost_estimate=COST,
        name="backward_rows",
    )(rows, gate, up, *weights)


def pair_sum_kernel(out_a, out_b, grad_a, grad_b, sum_ref):
    for begin, a_ref, b_ref in ((0, out_a, out_b), (SENT, grad_a, grad_b)):
        total = a_ref[...].astype(F32) + b_ref[...].astype(F32)
        sum_ref[:, begin : begin + SENT, :] = total.astype(BF16).reshape(CHIPS, SENT, D)


def pair_sum(*parts):
    return pl.pallas_call(
        pair_sum_kernel,
        out_shape=jax.ShapeDtypeStruct((CHIPS, 2 * SENT, D), BF16),
        in_specs=[VMEM] * 4,
        out_specs=VMEM,
        compiler_params=params(12),
        name="sum_halves",
    )(*parts)


def weight_grad_kernel(x_a, g_a, x_b, g_b, h_a, p_a, h_b, p_b, gate_ref, up_ref, down_ref):
    both = dot(x_a[...], p_a[...], 0, 0) + dot(x_b[...], p_b[...], 0, 0)
    gate_ref[0] = both[:, :HALF].astype(BF16)
    up_ref[0] = both[:, HALF:].astype(BF16)
    down_ref[0] = (dot(h_a[...], g_a[...], 0, 0) + dot(h_b[...], g_b[...], 0, 0)).astype(BF16)


def weight_grads(own_rows, own_grads, other_rows, other_grads, own_acts, other_acts):
    width = 512
    steps = D // width
    x_spec = pl.BlockSpec((ROWS, width), lambda i: (0, i))
    acts = [pl.BlockSpec((ROWS, HALF), lambda i: (0, 0)), pl.BlockSpec((ROWS, 2 * HALF), lambda i: (0, 0))]
    wide = pl.BlockSpec((1, width, HALF), lambda i: (0, i, 0))
    return pl.pallas_call(
        weight_grad_kernel,
        grid=(steps,),
        out_shape=(
            jax.ShapeDtypeStruct((1, D, HALF), BF16),
            jax.ShapeDtypeStruct((1, D, HALF), BF16),
            jax.ShapeDtypeStruct((1, HALF, D), BF16),
        ),
        in_specs=[x_spec] * 4 + acts + acts,
        out_specs=(wide, wide, pl.BlockSpec((1, HALF, width), lambda i: (0, 0, i))),
        compiler_params=params(20),
        cost_estimate=pl.CostEstimate(
            flops=12 * ROWS * D * HALF, bytes_accessed=12 * 2**20, transcendentals=0
        ),
        name="weight_grads",
    )(own_rows, own_grads, other_rows, other_grads, *own_acts, *other_acts)


def combine_kernel(first_ref, back_ref, all_ref, mask_ref, weight_ref, *out_refs):
    own, below2, above2, down_pair, up_pair, half, other_half = out_refs
    places = ((own, 0), (down_pair, TOK), (up_pair, TOK), (below2, 0), (above2, 0), (down_pair, 0), (up_pair, 0))

    def put(value, begin):
        value = value.astype(BF16)
        end = begin + value.shape[1]
        for j, (ref, row) in enumerate(places):
            ref[row : row + TOK, begin:end] = value[j * TOK : (j + 1) * TOK]
        if begin < D:
            half[:, begin:end] = value[GROUP - TOK :]
        else:
            other_half[:, begin - D : end - D] = value[GROUP - TOK :]

    mask = mask_ref[...]
    weight = weight_ref[...]
    high = weight.astype(BF16)
    low = (weight - high.astype(F32)).astype(BF16)
    products = jnp.zeros((GROUP, ROWS), F32)
    for i in range(0, D, 512):
        part = back_ref[:, :SENT, i : i + 512].reshape(ROWS, 512)
        put(dot(high, part, 1, 0) + dot(low, part, 1, 0), i)
        products = products + dot(all_ref[:, D + i : D + i + 512], part, 1, 1)
        put(dot(mask, back_ref[:, SENT:, i : i + 512].reshape(ROWS, 512), 1, 0), D + i)
    meta = all_ref[:, 2 * D :].astype(F32)
    products = products * mask.astype(F32)
    lane = lax.broadcasted_iota(jnp.int32, (GROUP, ROWS), 1)
    expert_of = (first_ref[0] + lane // (PLANES * SLOTS)).astype(F32)
    place = lax.broadcasted_iota(jnp.int32, (GROUP, META), 1)
    tail = jnp.zeros((GROUP, META), F32)
    for k in range(TOP):
        hit = meta[:, k : k + 1] == expert_of
        value = jnp.sum(jnp.where(hit, products, 0.0), axis=1, keepdims=True)
        for i, piece in enumerate(three_pieces(value)):
            tail = jnp.where(place == i * TOP + k, piece.astype(F32), tail)
    put(tail, 2 * D)


def combine(first, back, gathered, mask, weight):
    block = jax.ShapeDtypeStruct((TOK, COLS), BF16)
    pair = jax.ShapeDtypeStruct((2 * TOK, COLS), BF16)
    halves = (jax.ShapeDtypeStruct((TOK, D), BF16), jax.ShapeDtypeStruct((TOK, COLS - D), BF16))
    return pl.pallas_call(
        combine_kernel,
        out_shape=(block, block, block, pair, pair) + halves,
        in_specs=[SMEM] + [VMEM] * 4,
        out_specs=(VMEM,) * 7,
        compiler_params=params(10),
        name="combine_rows",
    )(first, back, gathered, mask, weight)


def relay_kernel(mine_up, next_up, first_half, mine_down, next_down, second_half, up_ref, down_ref):
    up = mine_up[...].astype(F32) + next_up[:TOK].astype(F32)
    up_ref[:, D:] = up[:, D:].astype(BF16)
    up_ref[:, :D] = (up[:, :D] + first_half[...].astype(F32)).astype(BF16)
    down = mine_down[...].astype(F32) + next_down[:TOK].astype(F32)
    down_ref[:, :D] = down[:, :D].astype(BF16)
    down_ref[:, D:] = (down[:, D:] + second_half[...].astype(F32)).astype(BF16)


def relay(*parts):
    block = jax.ShapeDtypeStruct((TOK, COLS), BF16)
    return pl.pallas_call(
        relay_kernel,
        out_shape=(block, block),
        in_specs=[VMEM] * 6,
        out_specs=(VMEM, VMEM),
        compiler_params=params(4),
        name="relay_rows",
    )(*parts)


def total_kernel(*refs):
    *in_refs, out_ref, grad_ref, route_ref = refs
    total = in_refs[0][...].astype(F32)
    for ref in in_refs[1:]:
        total = total + ref[ref.shape[0] - TOK :].astype(F32)
    out_ref[...] = total[:, :D].astype(BF16)
    grad_ref[...] = total[:, D : 2 * D].astype(BF16)
    tail = total[:, 2 * D :].T
    route_ref[...] = tail[:TOP] + tail[TOP : 2 * TOP] + tail[2 * TOP : 3 * TOP]


def totals(*parts):
    return pl.pallas_call(
        total_kernel,
        out_shape=(
            jax.ShapeDtypeStruct((TOK, D), BF16),
            jax.ShapeDtypeStruct((TOK, D), BF16),
            jax.ShapeDtypeStruct((TOP, TOK), F32),
        ),
        in_specs=[VMEM] * len(parts),
        out_specs=(VMEM, VMEM, VMEM),
        compiler_params=params(4),
        name="total_rows",
    )(*parts)


def swap_cores(value):
    return lax.ppermute(value, "core", [(0, 1), (1, 0)])


def over_plane(blocks):
    return lax.all_to_all(blocks, ("y", "x"), 0, 0, tiled=True)


def shift(value, step):
    return lax.ppermute(value, "z", [(i, (i + step) % PLANES) for i in range(PLANES)])


def spread_z(own, weights):
    below2, above2 = shift(own, 2), shift(own, -2)
    below, above = shift(own, 1), shift(own, -1)
    below2, above2, held = lax.optimization_barrier((below2, above2, hold(*weights)))
    half, other_half = shift(below2[:, :D], 2), shift(above2[:, D:], -2)
    below3, above3 = shift(below2, 1), shift(above2, -1)
    return (own, below, above, below2, above2, below3, above3, half, other_half), held


def reduce_z(own, below2, above2, down_pair, up_pair, half, other_half, beside):
    from_above, from_below = shift(down_pair, -1), shift(up_pair, 1)
    half, other_half = shift(half, 2), shift(other_half, -2)
    half, other_half, beside = lax.optimization_barrier((half, other_half, beside))
    up, down = relay(above2, from_below, half, below2, from_above, other_half)
    return totals(own, from_above, from_below, shift(up, 2), shift(down, -2)), beside


def body(tokens, expert_ids, route_weight, out_grad, gate_weight, up_weight, down_weight):
    first = (lax.axis_index("z") * CHIPS).astype(jnp.int32).reshape(1)
    first, tokens = lax.optimization_barrier((first, tokens))
    packed = pack(tokens, out_grad, expert_ids.T, route_weight.T)
    blocks, weights = spread_z(packed, (gate_weight, up_weight, down_weight))
    send, gathered, mask, weight = spread(first, blocks)
    arrived = over_plane(send)
    rows = arrived[:, :SENT].reshape(ROWS, D)
    grads = arrived[:, SENT:].reshape(ROWS, D)
    other_rows, other_grads = swap_cores(rows), swap_cores(grads)
    out_a, hidden_a, gate_a, up_a = forward(rows, weights)
    hidden_a, other_rows = lax.optimization_barrier((hidden_a, other_rows))
    out_b, hidden_b, gate_b, up_b = forward(other_rows, weights)
    grad_b, pre_b = backward(other_grads, gate_b, up_b, weights)
    from_b, gate_a = lax.optimization_barrier((swap_cores(out_b), gate_a))
    grad_a, pre_a = backward(grads, gate_a, up_a, weights)
    summed = pair_sum(out_a, from_b, grad_a, swap_cores(grad_b))
    back = over_plane(summed)
    back, pre_a = lax.optimization_barrier((back, pre_a))
    weight_out = weight_grads(rows, grads, other_rows, other_grads, (hidden_a, pre_a), (hidden_b, pre_b))
    (layer_out, token_grad, route_t), weight_out = reduce_z(
        *combine(first, back, gathered, mask, weight), beside=weight_out
    )
    return layer_out, token_grad, route_t.T, *weight_out


def solution(mesh):
    fine = Mesh(mesh.devices.reshape(SIZES), AXES)
    rows, pieces = P(AXES, None), P(AXES, None, None)
    return jax.shard_map(
        body,
        mesh=fine,
        in_specs=(rows, rows, rows, rows, pieces, pieces, pieces),
        out_specs=(rows, rows, rows, pieces, pieces, pieces),
        check_vma=False,
    )
```

```python
import functools

import jax
import jax.numpy as jnp
from jax import lax
from jax.experimental import pallas as pl
from jax.experimental.pallas import tpu as pltpu
from jax.sharding import Mesh, PartitionSpec as P

AXES = ("z", "y", "x", "core")
SIZES = (8, 4, 4, 2)
PLANES = 8
CHIPS = 16
TOK = 16
TOP = 8
SLOTS = 2
D = 2048
HALF = 384
META = 128
COLS = 2 * D + META
GROUP = PLANES * TOK
SENT = PLANES * SLOTS
ROWS = CHIPS * SENT
BLOCKS = PLANES + 1
F32 = jnp.float32
BF16 = jnp.bfloat16
VMEM = pl.BlockSpec(memory_space=pltpu.VMEM)
SMEM = pl.BlockSpec(memory_space=pltpu.SMEM)


def params(mib):
    return pltpu.CompilerParams(vmem_limit_bytes=mib * 2**20)


def dot(a, b, a_dim, b_dim):
    return lax.dot_general(a, b, (((a_dim,), (b_dim,)), ((), ())), preferred_element_type=F32)


def three_pieces(value):
    high = value.astype(BF16)
    rest = value - high.astype(F32)
    middle = rest.astype(BF16)
    low = (rest - middle.astype(F32)).astype(BF16)
    return high, middle, low


def pack_kernel(tok_hbm, grad_hbm, ids_hbm, weight_hbm, out_ref, ids_ref, weight_ref, sems):
    copies = [
        pltpu.make_async_copy(ids_hbm, ids_ref, sems.at[0]),
        pltpu.make_async_copy(weight_hbm, weight_ref, sems.at[1]),
        pltpu.make_async_copy(tok_hbm, out_ref.at[:, pl.ds(0, D)], sems.at[2]),
        pltpu.make_async_copy(grad_hbm, out_ref.at[:, pl.ds(D, D)], sems.at[3]),
    ]
    for copy in copies:
        copy.start()
    copies[0].wait()
    copies[1].wait()
    pieces = (ids_ref[...].astype(F32).astype(BF16),) + three_pieces(weight_ref[...])
    rows = lax.broadcasted_iota(jnp.int32, (TOP, META), 0)
    lanes = lax.broadcasted_iota(jnp.int32, (TOP, META), 1)
    meta = jnp.zeros((TOK, META), F32)
    for i, piece in enumerate(pieces):
        place = jnp.where(lanes == rows + i * TOP, 1.0, 0.0).astype(BF16)
        meta = meta + dot(piece, place, 0, 0)
    out_ref[:, 2 * D :] = meta.astype(BF16)
    copies[2].wait()
    copies[3].wait()


def pack(tokens, out_grad, ids_t, weight_t):
    return pl.pallas_call(
        pack_kernel,
        out_shape=jax.ShapeDtypeStruct((TOK, COLS), BF16),
        in_specs=[pl.BlockSpec(memory_space=pltpu.HBM)] * 4,
        out_specs=VMEM,
        scratch_shapes=[
            pltpu.VMEM((TOP, TOK), jnp.int32),
            pltpu.VMEM((TOP, TOK), F32),
            pltpu.SemaphoreType.DMA((4,)),
        ],
        compiler_params=params(63),
        name="pack_rows",
    )(tokens, out_grad, ids_t, weight_t)


def hold_kernel(gate_hbm, up_hbm, both_ref, sems):
    copies = [
        pltpu.make_async_copy(gate_hbm.at[0], both_ref.at[:, pl.ds(0, HALF)], sems.at[0]),
        pltpu.make_async_copy(up_hbm.at[0], both_ref.at[:, pl.ds(HALF, HALF)], sems.at[1]),
    ]
    for copy in copies:
        copy.start()
    for copy in copies:
        copy.wait()


def hold(gate_weight, up_weight):
    return pl.pallas_call(
        hold_kernel,
        out_shape=jax.ShapeDtypeStruct((D, 2 * HALF), BF16),
        in_specs=[pl.BlockSpec(memory_space=pltpu.HBM)] * 2,
        out_specs=VMEM,
        scratch_shapes=[pltpu.SemaphoreType.DMA((2,))],
        compiler_params=params(16),
        name="hold_weights",
    )(gate_weight, up_weight)


def spread_kernel(first_ref, *refs):
    blocks, (send_ref, all_ref, mask_ref, weight_ref) = refs[:BLOCKS], refs[BLOCKS:]
    for j, block in enumerate(blocks[:-1]):
        all_ref[min(j, PLANES - 1) * TOK : min(j, PLANES - 1) * TOK + TOK, : block.shape[1]] = block[...]
    all_ref[GROUP - TOK :, D:] = blocks[-1][...]
    meta = all_ref[:, 2 * D :].astype(F32)
    shape = (GROUP, ROWS)
    lane = lax.broadcasted_iota(jnp.int32, shape, 1)
    row = lax.broadcasted_iota(jnp.int32, shape, 0)
    expert = (first_ref[0] + lane // (PLANES * SLOTS)).astype(F32)
    named = jnp.zeros(shape, F32)
    weight = jnp.zeros(shape, F32)
    for k in range(TOP):
        hit = meta[:, k : k + 1] == expert
        w = meta[:, TOP + k : TOP + k + 1] + meta[:, 2 * TOP + k : 2 * TOP + k + 1]
        w = w + meta[:, 3 * TOP + k : 3 * TOP + k + 1]
        named = jnp.where(hit, 1.0, named)
        weight = jnp.where(hit, w, weight)
    ri = lax.broadcasted_iota(jnp.int32, (GROUP, GROUP), 0)
    ci = lax.broadcasted_iota(jnp.int32, (GROUP, GROUP), 1)
    earlier = jnp.where((ri // TOK == ci // TOK) & (ci < ri), 1.0, 0.0).astype(BF16)
    slot = dot(earlier, named.astype(BF16), 1, 0)
    wanted = (lane % SLOTS).astype(F32)
    source = (lane // SLOTS) % PLANES
    mask = jnp.where((slot == wanted) & (source == row // TOK), named, 0.0)
    weight = weight * mask
    mask_ref[...] = mask.astype(BF16)
    weight_ref[...] = weight
    pick = mask.T.astype(BF16)
    scale = jnp.sum(weight.T, axis=1, keepdims=True)
    for i in range(0, D, 512):
        picked = dot(pick, all_ref[:, i : i + 512], 1, 0)
        send_ref[:, :SENT, i : i + 512] = picked.astype(BF16).reshape(CHIPS, SENT, 512)
        picked = dot(pick, all_ref[:, D + i : D + i + 512], 1, 0) * scale
        send_ref[:, SENT:, i : i + 512] = picked.astype(BF16).reshape(CHIPS, SENT, 512)


def spread(first, blocks):
    return pl.pallas_call(
        spread_kernel,
        out_shape=(
            jax.ShapeDtypeStruct((CHIPS, 2 * SENT, D), BF16),
            jax.ShapeDtypeStruct((GROUP, COLS), BF16),
            jax.ShapeDtypeStruct((GROUP, ROWS), BF16),
            jax.ShapeDtypeStruct((GROUP, ROWS), F32),
        ),
        in_specs=[SMEM] + [VMEM] * BLOCKS,
        out_specs=(VMEM,) * 4,
        compiler_params=params(10),
        name="spread_rows",
    )(first, *blocks)


def forward_kernel(in_ref, both_ref, down_ref, back_ref, hidden_ref, gate_out, up_out):
    rows = in_ref[...]
    gate = dot(rows, both_ref[:, :HALF], 1, 0)
    up = dot(rows, both_ref[:, HALF:], 1, 0)
    gate_out[...] = gate
    up_out[...] = up
    hidden = (gate * jax.nn.sigmoid(gate) * up).astype(BF16)
    hidden_ref[...] = hidden
    for i in range(0, D, 512):
        back_ref[:, i : i + 512] = dot(hidden, down_ref[0, :, i : i + 512], 1, 0).astype(BF16)


def backward_kernel(in_ref, gate_in, up_in, both_ref, down_ref, back_ref, pre_ref):
    gate = gate_in[...]
    sig = jax.nn.sigmoid(gate)
    hidden_grad = dot(in_ref[...], down_ref[0], 1, 1)
    pre_ref[:, :HALF] = (hidden_grad * up_in[...] * sig * (1.0 + gate * (1.0 - sig))).astype(BF16)
    pre_ref[:, HALF:] = (hidden_grad * gate * sig).astype(BF16)
    for i in range(0, D, 512):
        back_ref[:, i : i + 512] = dot(pre_ref[...], both_ref[i : i + 512, :], 1, 1).astype(BF16)


COST = pl.CostEstimate(flops=6 * ROWS * D * HALF, bytes_accessed=5 * 2**20, transcendentals=ROWS * HALF)
WIDE = jax.ShapeDtypeStruct((ROWS, D), BF16)
ACT = jax.ShapeDtypeStruct((ROWS, HALF), BF16)
ACT32 = jax.ShapeDtypeStruct((ROWS, HALF), F32)


def forward(rows, weights):
    return pl.pallas_call(
        forward_kernel,
        out_shape=(WIDE, ACT, ACT32, ACT32),
        in_specs=[VMEM] * 3,
        out_specs=(VMEM,) * 4,
        compiler_params=params(16),
        cost_estimate=COST,
        name="forward_rows",
    )(rows, *weights)


def backward(rows, gate, up, weights):
    return pl.pallas_call(
        backward_kernel,
        out_shape=(WIDE, jax.ShapeDtypeStruct((ROWS, 2 * HALF), BF16)),
        in_specs=[VMEM] * 5,
        out_specs=(VMEM,) * 2,
        compiler_params=params(16),
        cost_estimate=COST,
        name="backward_rows",
    )(rows, gate, up, *weights)


def pair_sum_kernel(out_a, out_b, grad_a, grad_b, sum_ref):
    for begin, a_ref, b_ref in ((0, out_a, out_b), (SENT, grad_a, grad_b)):
        total = a_ref[...].astype(F32) + b_ref[...].astype(F32)
        sum_ref[:, begin : begin + SENT, :] = total.astype(BF16).reshape(CHIPS, SENT, D)


def pair_sum(*parts):
    return pl.pallas_call(
        pair_sum_kernel,
        out_shape=jax.ShapeDtypeStruct((CHIPS, 2 * SENT, D), BF16),
        in_specs=[VMEM] * 4,
        out_specs=VMEM,
        compiler_params=params(12),
        name="sum_halves",
    )(*parts)


def weight_grad_kernel(x_a, g_a, x_b, g_b, h_a, p_a, h_b, p_b, gate_ref, up_ref, down_ref):
    both = dot(x_a[...], p_a[...], 0, 0) + dot(x_b[...], p_b[...], 0, 0)
    gate_ref[0] = both[:, :HALF].astype(BF16)
    up_ref[0] = both[:, HALF:].astype(BF16)
    down_ref[0] = (dot(h_a[...], g_a[...], 0, 0) + dot(h_b[...], g_b[...], 0, 0)).astype(BF16)


def weight_grads(own_rows, own_grads, other_rows, other_grads, own_acts, other_acts):
    width = 512
    steps = D // width
    x_spec = pl.BlockSpec((ROWS, width), lambda i: (0, i))
    acts = [pl.BlockSpec((ROWS, HALF), lambda i: (0, 0)), pl.BlockSpec((ROWS, 2 * HALF), lambda i: (0, 0))]
    wide = pl.BlockSpec((1, width, HALF), lambda i: (0, i, 0))
    return pl.pallas_call(
        weight_grad_kernel,
        grid=(steps,),
        out_shape=(
            jax.ShapeDtypeStruct((1, D, HALF), BF16),
            jax.ShapeDtypeStruct((1, D, HALF), BF16),
            jax.ShapeDtypeStruct((1, HALF, D), BF16),
        ),
        in_specs=[x_spec] * 4 + acts + acts,
        out_specs=(wide, wide, pl.BlockSpec((1, HALF, width), lambda i: (0, 0, i))),
        compiler_params=params(20),
        cost_estimate=pl.CostEstimate(
            flops=12 * ROWS * D * HALF, bytes_accessed=12 * 2**20, transcendentals=0
        ),
        name="weight_grads",
    )(own_rows, own_grads, other_rows, other_grads, *own_acts, *other_acts)


def combine_kernel(first_ref, back_ref, all_ref, mask_ref, weight_ref, *out_refs):
    own, below2, above2, down_pair, up_pair, half, other_half = out_refs
    places = ((own, 0), (down_pair, TOK), (up_pair, TOK), (below2, 0), (above2, 0), (down_pair, 0), (up_pair, 0))

    def put(value, begin):
        value = value.astype(BF16)
        end = begin + value.shape[1]
        for j, (ref, row) in enumerate(places):
            ref[row : row + TOK, begin:end] = value[j * TOK : (j + 1) * TOK]
        if begin < D:
            half[:, begin:end] = value[GROUP - TOK :]
        else:
            other_half[:, begin - D : end - D] = value[GROUP - TOK :]

    mask = mask_ref[...]
    weight = weight_ref[...]
    high = weight.astype(BF16)
    low = (weight - high.astype(F32)).astype(BF16)
    products = jnp.zeros((GROUP, ROWS), F32)
    for i in range(0, D, 512):
        part = back_ref[:, :SENT, i : i + 512].reshape(ROWS, 512)
        put(dot(high, part, 1, 0) + dot(low, part, 1, 0), i)
        products = products + dot(all_ref[:, D + i : D + i + 512], part, 1, 1)
        put(dot(mask, back_ref[:, SENT:, i : i + 512].reshape(ROWS, 512), 1, 0), D + i)
    meta = all_ref[:, 2 * D :].astype(F32)
    products = products * mask.astype(F32)
    lane = lax.broadcasted_iota(jnp.int32, (GROUP, ROWS), 1)
    expert_of = (first_ref[0] + lane // (PLANES * SLOTS)).astype(F32)
    place = lax.broadcasted_iota(jnp.int32, (GROUP, META), 1)
    tail = jnp.zeros((GROUP, META), F32)
    for k in range(TOP):
        hit = meta[:, k : k + 1] == expert_of
        value = jnp.sum(jnp.where(hit, products, 0.0), axis=1, keepdims=True)
        for i, piece in enumerate(three_pieces(value)):
            tail = jnp.where(place == i * TOP + k, piece.astype(F32), tail)
    put(tail, 2 * D)


def combine(first, back, gathered, mask, weight):
    block = jax.ShapeDtypeStruct((TOK, COLS), BF16)
    pair = jax.ShapeDtypeStruct((2 * TOK, COLS), BF16)
    halves = (jax.ShapeDtypeStruct((TOK, D), BF16), jax.ShapeDtypeStruct((TOK, COLS - D), BF16))
    return pl.pallas_call(
        combine_kernel,
        out_shape=(block, block, block, pair, pair) + halves,
        in_specs=[SMEM] + [VMEM] * 4,
        out_specs=(VMEM,) * 7,
        compiler_params=params(10),
        name="combine_rows",
    )(first, back, gathered, mask, weight)


def relay_kernel(mine_up, next_up, first_half, mine_down, next_down, second_half, up_ref, down_ref):
    up = mine_up[...].astype(F32) + next_up[:TOK].astype(F32)
    up_ref[:, D:] = up[:, D:].astype(BF16)
    up_ref[:, :D] = (up[:, :D] + first_half[...].astype(F32)).astype(BF16)
    down = mine_down[...].astype(F32) + next_down[:TOK].astype(F32)
    down_ref[:, :D] = down[:, :D].astype(BF16)
    down_ref[:, D:] = (down[:, D:] + second_half[...].astype(F32)).astype(BF16)


def relay(*parts):
    block = jax.ShapeDtypeStruct((TOK, COLS), BF16)
    return pl.pallas_call(
        relay_kernel,
        out_shape=(block, block),
        in_specs=[VMEM] * 6,
        out_specs=(VMEM, VMEM),
        compiler_params=params(4),
        name="relay_rows",
    )(*parts)


def total_kernel(*refs):
    *in_refs, out_ref, grad_ref, route_ref = refs
    total = in_refs[0][...].astype(F32)
    for ref in in_refs[1:]:
        total = total + ref[ref.shape[0] - TOK :].astype(F32)
    out_ref[...] = total[:, :D].astype(BF16)
    grad_ref[...] = total[:, D : 2 * D].astype(BF16)
    tail = total[:, 2 * D :].T
    route_ref[...] = tail[:TOP] + tail[TOP : 2 * TOP] + tail[2 * TOP : 3 * TOP]


def totals(*parts):
    return pl.pallas_call(
        total_kernel,
        out_shape=(
            jax.ShapeDtypeStruct((TOK, D), BF16),
            jax.ShapeDtypeStruct((TOK, D), BF16),
            jax.ShapeDtypeStruct((TOP, TOK), F32),
        ),
        in_specs=[VMEM] * len(parts),
        out_specs=(VMEM, VMEM, VMEM),
        compiler_params=params(4),
        name="total_rows",
    )(*parts)


def swap_cores(value):
    return lax.ppermute(value, "core", [(0, 1), (1, 0)])


def over_plane(blocks):
    return lax.all_to_all(blocks, ("y", "x"), 0, 0, tiled=True)


def shift(value, step):
    return lax.ppermute(value, "z", [(i, (i + step) % PLANES) for i in range(PLANES)])


def spread_z(own, weights):
    below2, above2 = shift(own, 2), shift(own, -2)
    below, above = shift(own, 1), shift(own, -1)
    below2, above2, held = lax.optimization_barrier((below2, above2, hold(*weights)))
    half, other_half = shift(below2[:, :D], 2), shift(above2[:, D:], -2)
    below3, above3 = shift(below2, 1), shift(above2, -1)
    return (own, below, above, below2, above2, below3, above3, half, other_half), held


def reduce_z(own, below2, above2, down_pair, up_pair, half, other_half, beside):
    from_above, from_below = shift(down_pair, -1), shift(up_pair, 1)
    half, other_half = shift(half, 2), shift(other_half, -2)
    half, other_half, beside = lax.optimization_barrier((half, other_half, beside))
    up, down = relay(above2, from_below, half, below2, from_above, other_half)
    return totals(own, from_above, from_below, shift(up, 2), shift(down, -2)), beside


def body(tokens, expert_ids, route_weight, out_grad, gate_weight, up_weight, down_weight):
    first = (lax.axis_index("z") * CHIPS).astype(jnp.int32).reshape(1)
    first, tokens = lax.optimization_barrier((first, tokens))
    packed = pack(tokens, out_grad, expert_ids.T, route_weight.T)
    blocks, both = spread_z(packed, (gate_weight, up_weight))
    weights = (both, down_weight)
    send, gathered, mask, weight = spread(first, blocks)
    arrived = over_plane(send)
    rows = arrived[:, :SENT].reshape(ROWS, D)
    grads = arrived[:, SENT:].reshape(ROWS, D)
    other_rows, other_grads = swap_cores(rows), swap_cores(grads)
    out_a, hidden_a, gate_a, up_a = forward(rows, weights)
    hidden_a, other_rows = lax.optimization_barrier((hidden_a, other_rows))
    out_b, hidden_b, gate_b, up_b = forward(other_rows, weights)
    grad_b, pre_b = backward(other_grads, gate_b, up_b, weights)
    from_b, gate_a = lax.optimization_barrier((swap_cores(out_b), gate_a))
    grad_a, pre_a = backward(grads, gate_a, up_a, weights)
    summed = pair_sum(out_a, from_b, grad_a, swap_cores(grad_b))
    back = over_plane(summed)
    back, pre_a = lax.optimization_barrier((back, pre_a))
    weight_out = weight_grads(rows, grads, other_rows, other_grads, (hidden_a, pre_a), (hidden_b, pre_b))
    (layer_out, token_grad, route_t), weight_out = reduce_z(
        *combine(first, back, gathered, mask, weight), beside=weight_out
    )
    return layer_out, token_grad, route_t.T, *weight_out


def solution(mesh):
    fine = Mesh(mesh.devices.reshape(SIZES), AXES)
    rows, pieces = P(AXES, None), P(AXES, None, None)
    return jax.shard_map(
        body,
        mesh=fine,
        in_specs=(rows, rows, rows, rows, pieces, pieces, pieces),
        out_specs=(rows, rows, rows, pieces, pieces, pieces),
        check_vma=False,
    )
```

```python
import functools

import jax
import jax.numpy as jnp
from jax import lax
from jax.experimental import pallas as pl
from jax.experimental.pallas import tpu as pltpu
from jax.sharding import Mesh, PartitionSpec as P

AXES = ("z", "y", "x", "core")
SIZES = (8, 4, 4, 2)
PLANES = 8
CHIPS = 16
TOK = 16
TOP = 8
SLOTS = 2
D = 2048
HALF = 384
META = 128
COLS = 2 * D + META
GROUP = PLANES * TOK
SENT = PLANES * SLOTS
ROWS = CHIPS * SENT
BLOCKS = PLANES + 1
F32 = jnp.float32
BF16 = jnp.bfloat16
VMEM = pl.BlockSpec(memory_space=pltpu.VMEM)
SMEM = pl.BlockSpec(memory_space=pltpu.SMEM)


def params(mib):
    return pltpu.CompilerParams(vmem_limit_bytes=mib * 2**20)


def dot(a, b, a_dim, b_dim):
    return lax.dot_general(a, b, (((a_dim,), (b_dim,)), ((), ())), preferred_element_type=F32)


def three_pieces(value):
    high = value.astype(BF16)
    rest = value - high.astype(F32)
    middle = rest.astype(BF16)
    low = (rest - middle.astype(F32)).astype(BF16)
    return high, middle, low


def pack_kernel(tok_hbm, grad_hbm, ids_hbm, weight_hbm, out_ref, ids_ref, weight_ref, sems):
    copies = [
        pltpu.make_async_copy(ids_hbm, ids_ref, sems.at[0]),
        pltpu.make_async_copy(weight_hbm, weight_ref, sems.at[1]),
        pltpu.make_async_copy(tok_hbm, out_ref.at[:, pl.ds(0, D)], sems.at[2]),
        pltpu.make_async_copy(grad_hbm, out_ref.at[:, pl.ds(D, D)], sems.at[3]),
    ]
    for copy in copies:
        copy.start()
    copies[0].wait()
    copies[1].wait()
    pieces = (ids_ref[...].astype(F32).astype(BF16),) + three_pieces(weight_ref[...])
    rows = lax.broadcasted_iota(jnp.int32, (TOP, META), 0)
    lanes = lax.broadcasted_iota(jnp.int32, (TOP, META), 1)
    meta = jnp.zeros((TOK, META), F32)
    for i, piece in enumerate(pieces):
        place = jnp.where(lanes == rows + i * TOP, 1.0, 0.0).astype(BF16)
        meta = meta + dot(piece, place, 0, 0)
    out_ref[:, 2 * D :] = meta.astype(BF16)
    copies[2].wait()
    copies[3].wait()


def pack(tokens, out_grad, ids_t, weight_t):
    return pl.pallas_call(
        pack_kernel,
        out_shape=jax.ShapeDtypeStruct((TOK, COLS), BF16),
        in_specs=[pl.BlockSpec(memory_space=pltpu.HBM)] * 4,
        out_specs=VMEM,
        scratch_shapes=[
            pltpu.VMEM((TOP, TOK), jnp.int32),
            pltpu.VMEM((TOP, TOK), F32),
            pltpu.SemaphoreType.DMA((4,)),
        ],
        compiler_params=params(63),
        name="pack_rows",
    )(tokens, out_grad, ids_t, weight_t)


def hold_kernel(gate_hbm, up_hbm, both_ref, sems):
    copies = [
        pltpu.make_async_copy(gate_hbm.at[0], both_ref.at[:, pl.ds(0, HALF)], sems.at[0]),
        pltpu.make_async_copy(up_hbm.at[0], both_ref.at[:, pl.ds(HALF, HALF)], sems.at[1]),
    ]
    for copy in copies:
        copy.start()
    for copy in copies:
        copy.wait()


def hold(gate_weight, up_weight):
    return pl.pallas_call(
        hold_kernel,
        out_shape=jax.ShapeDtypeStruct((D, 2 * HALF), BF16),
        in_specs=[pl.BlockSpec(memory_space=pltpu.HBM)] * 2,
        out_specs=VMEM,
        scratch_shapes=[pltpu.SemaphoreType.DMA((2,))],
        compiler_params=params(16),
        name="hold_weights",
    )(gate_weight, up_weight)


def spread_kernel(first_ref, *refs):
    blocks, (send_ref, all_ref, mask_ref, weight_ref) = refs[:BLOCKS], refs[BLOCKS:]
    for j, block in enumerate(blocks[:-1]):
        all_ref[min(j, PLANES - 1) * TOK : min(j, PLANES - 1) * TOK + TOK, : block.shape[1]] = block[...]
    all_ref[GROUP - TOK :, D:] = blocks[-1][...]
    meta = all_ref[:, 2 * D :].astype(F32)
    shape = (GROUP, ROWS)
    lane = lax.broadcasted_iota(jnp.int32, shape, 1)
    row = lax.broadcasted_iota(jnp.int32, shape, 0)
    expert = (first_ref[0] + lane // (PLANES * SLOTS)).astype(F32)
    named = jnp.zeros(shape, F32)
    weight = jnp.zeros(shape, F32)
    for k in range(TOP):
        hit = meta[:, k : k + 1] == expert
        w = meta[:, TOP + k : TOP + k + 1] + meta[:, 2 * TOP + k : 2 * TOP + k + 1]
        w = w + meta[:, 3 * TOP + k : 3 * TOP + k + 1]
        named = jnp.where(hit, 1.0, named)
        weight = jnp.where(hit, w, weight)
    ri = lax.broadcasted_iota(jnp.int32, (GROUP, GROUP), 0)
    ci = lax.broadcasted_iota(jnp.int32, (GROUP, GROUP), 1)
    earlier = jnp.where((ri // TOK == ci // TOK) & (ci < ri), 1.0, 0.0).astype(BF16)
    slot = dot(earlier, named.astype(BF16), 1, 0)
    wanted = (lane % SLOTS).astype(F32)
    source = (lane // SLOTS) % PLANES
    mask = jnp.where((slot == wanted) & (source == row // TOK), named, 0.0)
    weight = weight * mask
    mask_ref[...] = mask.astype(BF16)
    weight_ref[...] = weight
    pick = mask.T.astype(BF16)
    scale = jnp.sum(weight.T, axis=1, keepdims=True)
    for i in range(0, D, 512):
        picked = dot(pick, all_ref[:, i : i + 512], 1, 0)
        send_ref[:, :SENT, i : i + 512] = picked.astype(BF16).reshape(CHIPS, SENT, 512)
        picked = dot(pick, all_ref[:, D + i : D + i + 512], 1, 0) * scale
        send_ref[:, SENT:, i : i + 512] = picked.astype(BF16).reshape(CHIPS, SENT, 512)


def spread(first, blocks):
    return pl.pallas_call(
        spread_kernel,
        out_shape=(
            jax.ShapeDtypeStruct((CHIPS, 2 * SENT, D), BF16),
            jax.ShapeDtypeStruct((GROUP, COLS), BF16),
            jax.ShapeDtypeStruct((GROUP, ROWS), BF16),
            jax.ShapeDtypeStruct((GROUP, ROWS), F32),
        ),
        in_specs=[SMEM] + [VMEM] * BLOCKS,
        out_specs=(VMEM,) * 4,
        compiler_params=params(10),
        name="spread_rows",
    )(first, *blocks)


def forward_kernel(in_ref, both_ref, down_ref, back_ref, hidden_ref, gate_out, up_out):
    rows = in_ref[...]
    gate = dot(rows, both_ref[:, :HALF], 1, 0)
    up = dot(rows, both_ref[:, HALF:], 1, 0)
    gate_out[...] = gate
    up_out[...] = up
    hidden = (gate * jax.nn.sigmoid(gate) * up).astype(BF16)
    hidden_ref[...] = hidden
    for i in range(0, D, 512):
        back_ref[:, i : i + 512] = dot(hidden, down_ref[0, :, i : i + 512], 1, 0).astype(BF16)


def backward_kernel(in_ref, gate_in, up_in, both_ref, down_ref, back_ref, pre_ref):
    gate = gate_in[...]
    sig = jax.nn.sigmoid(gate)
    hidden_grad = dot(in_ref[...], down_ref[0], 1, 1)
    pre_ref[:, :HALF] = (hidden_grad * up_in[...] * sig * (1.0 + gate * (1.0 - sig))).astype(BF16)
    pre_ref[:, HALF:] = (hidden_grad * gate * sig).astype(BF16)
    for i in range(0, D, 512):
        back_ref[:, i : i + 512] = dot(pre_ref[...], both_ref[i : i + 512, :], 1, 1).astype(BF16)


COST = pl.CostEstimate(flops=6 * ROWS * D * HALF, bytes_accessed=5 * 2**20, transcendentals=ROWS * HALF)
WIDE = jax.ShapeDtypeStruct((ROWS, D), BF16)
ACT = jax.ShapeDtypeStruct((ROWS, HALF), BF16)
ACT32 = jax.ShapeDtypeStruct((ROWS, HALF), F32)


def forward(rows, weights):
    return pl.pallas_call(
        forward_kernel,
        out_shape=(WIDE, ACT, ACT32, ACT32),
        in_specs=[VMEM] * 3,
        out_specs=(VMEM,) * 4,
        compiler_params=params(16),
        cost_estimate=COST,
        name="forward_rows",
    )(rows, *weights)


def backward(rows, gate, up, weights):
    return pl.pallas_call(
        backward_kernel,
        out_shape=(WIDE, jax.ShapeDtypeStruct((ROWS, 2 * HALF), BF16)),
        in_specs=[VMEM] * 5,
        out_specs=(VMEM,) * 2,
        compiler_params=params(16),
        cost_estimate=COST,
        name="backward_rows",
    )(rows, gate, up, *weights)


def pair_sum_kernel(out_a, out_b, grad_a, grad_b, sum_ref):
    for begin, a_ref, b_ref in ((0, out_a, out_b), (SENT, grad_a, grad_b)):
        total = a_ref[...].astype(F32) + b_ref[...].astype(F32)
        sum_ref[:, begin : begin + SENT, :] = total.astype(BF16).reshape(CHIPS, SENT, D)


def pair_sum(*parts):
    return pl.pallas_call(
        pair_sum_kernel,
        out_shape=jax.ShapeDtypeStruct((CHIPS, 2 * SENT, D), BF16),
        in_specs=[VMEM] * 4,
        out_specs=VMEM,
        compiler_params=params(12),
        name="sum_halves",
    )(*parts)


def weight_grad_kernel(x_a, g_a, x_b, g_b, h_a, p_a, h_b, p_b, gate_ref, up_ref, down_ref):
    both = dot(x_a[...], p_a[...], 0, 0) + dot(x_b[...], p_b[...], 0, 0)
    gate_ref[0] = both[:, :HALF].astype(BF16)
    up_ref[0] = both[:, HALF:].astype(BF16)
    down_ref[0] = (dot(h_a[...], g_a[...], 0, 0) + dot(h_b[...], g_b[...], 0, 0)).astype(BF16)


def weight_grads(own_rows, own_grads, other_rows, other_grads, own_acts, other_acts):
    width = 512
    steps = D // width
    x_spec = pl.BlockSpec((ROWS, width), lambda i: (0, i))
    acts = [pl.BlockSpec((ROWS, HALF), lambda i: (0, 0)), pl.BlockSpec((ROWS, 2 * HALF), lambda i: (0, 0))]
    wide = pl.BlockSpec((1, width, HALF), lambda i: (0, i, 0))
    return pl.pallas_call(
        weight_grad_kernel,
        grid=(steps,),
        out_shape=(
            jax.ShapeDtypeStruct((1, D, HALF), BF16),
            jax.ShapeDtypeStruct((1, D, HALF), BF16),
            jax.ShapeDtypeStruct((1, HALF, D), BF16),
        ),
        in_specs=[x_spec] * 4 + acts + acts,
        out_specs=(wide, wide, pl.BlockSpec((1, HALF, width), lambda i: (0, 0, i))),
        compiler_params=params(20),
        cost_estimate=pl.CostEstimate(
            flops=12 * ROWS * D * HALF, bytes_accessed=12 * 2**20, transcendentals=0
        ),
        name="weight_grads",
    )(own_rows, own_grads, other_rows, other_grads, *own_acts, *other_acts)


def combine_kernel(first_ref, back_ref, all_ref, mask_ref, weight_ref, *out_refs):
    own, below2, above2, down_pair, up_pair, half, other_half = out_refs
    places = ((own, 0), (down_pair, TOK), (up_pair, TOK), (below2, 0), (above2, 0), (down_pair, 0), (up_pair, 0))

    def put(value, begin):
        value = value.astype(BF16)
        end = begin + value.shape[1]
        for j, (ref, row) in enumerate(places):
            ref[row : row + TOK, begin:end] = value[j * TOK : (j + 1) * TOK]
        if begin < D:
            half[:, begin:end] = value[GROUP - TOK :]
        else:
            other_half[:, begin - D : end - D] = value[GROUP - TOK :]

    mask = mask_ref[...]
    weight = weight_ref[...]
    high = weight.astype(BF16)
    low = (weight - high.astype(F32)).astype(BF16)
    both = jnp.concatenate([high, low], axis=0)
    products = jnp.zeros((GROUP, ROWS), F32)
    for i in range(0, D, 512):
        part = back_ref[:, :SENT, i : i + 512].reshape(ROWS, 512)
        total = dot(both, part, 1, 0)
        put(total[:GROUP] + total[GROUP:], i)
        products = products + dot(all_ref[:, D + i : D + i + 512], part, 1, 1)
        put(dot(mask, back_ref[:, SENT:, i : i + 512].reshape(ROWS, 512), 1, 0), D + i)
    meta = all_ref[:, 2 * D :].astype(F32)
    products = products * mask.astype(F32)
    lane = lax.broadcasted_iota(jnp.int32, (GROUP, ROWS), 1)
    expert_of = (first_ref[0] + lane // (PLANES * SLOTS)).astype(F32)
    place = lax.broadcasted_iota(jnp.int32, (GROUP, META), 1)
    tail = jnp.zeros((GROUP, META), F32)
    for k in range(TOP):
        hit = meta[:, k : k + 1] == expert_of
        value = jnp.sum(jnp.where(hit, products, 0.0), axis=1, keepdims=True)
        for i, piece in enumerate(three_pieces(value)):
            tail = jnp.where(place == i * TOP + k, piece.astype(F32), tail)
    put(tail, 2 * D)


def combine(first, back, gathered, mask, weight):
    block = jax.ShapeDtypeStruct((TOK, COLS), BF16)
    pair = jax.ShapeDtypeStruct((2 * TOK, COLS), BF16)
    halves = (jax.ShapeDtypeStruct((TOK, D), BF16), jax.ShapeDtypeStruct((TOK, COLS - D), BF16))
    return pl.pallas_call(
        combine_kernel,
        out_shape=(block, block, block, pair, pair) + halves,
        in_specs=[SMEM] + [VMEM] * 4,
        out_specs=(VMEM,) * 7,
        compiler_params=params(10),
        name="combine_rows",
    )(first, back, gathered, mask, weight)


def relay_kernel(mine_up, next_up, first_half, mine_down, next_down, second_half, up_ref, down_ref):
    up = mine_up[...].astype(F32) + next_up[:TOK].astype(F32)
    up_ref[:, D:] = up[:, D:].astype(BF16)
    up_ref[:, :D] = (up[:, :D] + first_half[...].astype(F32)).astype(BF16)
    down = mine_down[...].astype(F32) + next_down[:TOK].astype(F32)
    down_ref[:, :D] = down[:, :D].astype(BF16)
    down_ref[:, D:] = (down[:, D:] + second_half[...].astype(F32)).astype(BF16)


def relay(*parts):
    block = jax.ShapeDtypeStruct((TOK, COLS), BF16)
    return pl.pallas_call(
        relay_kernel,
        out_shape=(block, block),
        in_specs=[VMEM] * 6,
        out_specs=(VMEM, VMEM),
        compiler_params=params(4),
        name="relay_rows",
    )(*parts)


def total_kernel(*refs):
    *in_refs, out_ref, grad_ref, route_ref = refs
    total = in_refs[0][...].astype(F32)
    for ref in in_refs[1:]:
        total = total + ref[ref.shape[0] - TOK :].astype(F32)
    out_ref[...] = total[:, :D].astype(BF16)
    grad_ref[...] = total[:, D : 2 * D].astype(BF16)
    tail = total[:, 2 * D :].T
    route_ref[...] = tail[:TOP] + tail[TOP : 2 * TOP] + tail[2 * TOP : 3 * TOP]


def totals(*parts):
    return pl.pallas_call(
        total_kernel,
        out_shape=(
            jax.ShapeDtypeStruct((TOK, D), BF16),
            jax.ShapeDtypeStruct((TOK, D), BF16),
            jax.ShapeDtypeStruct((TOP, TOK), F32),
        ),
        in_specs=[VMEM] * len(parts),
        out_specs=(VMEM, VMEM, VMEM),
        compiler_params=params(4),
        name="total_rows",
    )(*parts)


def swap_cores(value):
    return lax.ppermute(value, "core", [(0, 1), (1, 0)])


def over_plane(blocks):
    return lax.all_to_all(blocks, ("y", "x"), 0, 0, tiled=True)


def shift(value, step):
    return lax.ppermute(value, "z", [(i, (i + step) % PLANES) for i in range(PLANES)])


def spread_z(own, weights):
    below2, above2 = shift(own, 2), shift(own, -2)
    below, above = shift(own, 1), shift(own, -1)
    above2, held = lax.optimization_barrier((above2, hold(*weights)))
    half, other_half = shift(below2[:, :D], 2), shift(above2[:, D:], -2)
    below3, above3 = shift(below2, 1), shift(above2, -1)
    return (own, below, above, below2, above2, below3, above3, half, other_half), held


def reduce_z(own, below2, above2, down_pair, up_pair, half, other_half, beside):
    from_above, from_below = shift(down_pair, -1), shift(up_pair, 1)
    half, other_half = shift(half, 2), shift(other_half, -2)
    half, other_half, beside = lax.optimization_barrier((half, other_half, beside))
    up, down = relay(above2, from_below, half, below2, from_above, other_half)
    return totals(own, from_above, from_below, shift(up, 2), shift(down, -2)), beside


def body(tokens, expert_ids, route_weight, out_grad, gate_weight, up_weight, down_weight):
    first = (lax.axis_index("z") * CHIPS).astype(jnp.int32).reshape(1)
    first, tokens = lax.optimization_barrier((first, tokens))
    packed = pack(tokens, out_grad, expert_ids.T, route_weight.T)
    blocks, both = spread_z(packed, (gate_weight, up_weight))
    weights = (both, down_weight)
    send, gathered, mask, weight = spread(first, blocks)
    arrived = over_plane(send)
    rows = arrived[:, :SENT].reshape(ROWS, D)
    grads = arrived[:, SENT:].reshape(ROWS, D)
    other_rows, other_grads = swap_cores(rows), swap_cores(grads)
    out_a, hidden_a, gate_a, up_a = forward(rows, weights)
    hidden_a, other_rows = lax.optimization_barrier((hidden_a, other_rows))
    out_b, hidden_b, gate_b, up_b = forward(other_rows, weights)
    grad_b, pre_b = backward(other_grads, gate_b, up_b, weights)
    from_b, gate_a = lax.optimization_barrier((swap_cores(out_b), gate_a))
    grad_a, pre_a = backward(grads, gate_a, up_a, weights)
    summed = pair_sum(out_a, from_b, grad_a, swap_cores(grad_b))
    back = over_plane(summed)
    back, pre_a = lax.optimization_barrier((back, pre_a))
    weight_out = weight_grads(rows, grads, other_rows, other_grads, (hidden_a, pre_a), (hidden_b, pre_b))
    (layer_out, token_grad, route_t), weight_out = reduce_z(
        *combine(first, back, gathered, mask, weight), beside=weight_out
    )
    return layer_out, token_grad, route_t.T, *weight_out


def solution(mesh):
    fine = Mesh(mesh.devices.reshape(SIZES), AXES)
    rows, pieces = P(AXES, None), P(AXES, None, None)
    return jax.shard_map(
        body,
        mesh=fine,
        in_specs=(rows, rows, rows, rows, pieces, pieces, pieces),
        out_specs=(rows, rows, rows, pieces, pieces, pieces),
        check_vma=False,
    )
```

```python
import functools

import jax
import jax.numpy as jnp
from jax import lax
from jax.experimental import pallas as pl
from jax.experimental.pallas import tpu as pltpu
from jax.sharding import Mesh, PartitionSpec as P

AXES = ("z", "y", "x", "core")
SIZES = (8, 4, 4, 2)
PLANES = 8
CHIPS = 16
TOK = 16
TOP = 8
SLOTS = 2
D = 2048
HALF = 384
META = 128
COLS = 2 * D + META
GROUP = PLANES * TOK
SENT = PLANES * SLOTS
ROWS = CHIPS * SENT
BLOCKS = PLANES + 1
F32 = jnp.float32
BF16 = jnp.bfloat16
VMEM = pl.BlockSpec(memory_space=pltpu.VMEM)
SMEM = pl.BlockSpec(memory_space=pltpu.SMEM)


def params(mib):
    return pltpu.CompilerParams(vmem_limit_bytes=mib * 2**20)


def dot(a, b, a_dim, b_dim):
    return lax.dot_general(a, b, (((a_dim,), (b_dim,)), ((), ())), preferred_element_type=F32)


def three_pieces(value):
    high = value.astype(BF16)
    rest = value - high.astype(F32)
    middle = rest.astype(BF16)
    low = (rest - middle.astype(F32)).astype(BF16)
    return high, middle, low


def pack_kernel(tok_hbm, grad_hbm, ids_hbm, weight_hbm, out_ref, ids_ref, weight_ref, sems):
    copies = [
        pltpu.make_async_copy(ids_hbm, ids_ref, sems.at[0]),
        pltpu.make_async_copy(weight_hbm, weight_ref, sems.at[1]),
        pltpu.make_async_copy(tok_hbm, out_ref.at[:, pl.ds(0, D)], sems.at[2]),
        pltpu.make_async_copy(grad_hbm, out_ref.at[:, pl.ds(D, D)], sems.at[3]),
    ]
    for copy in copies:
        copy.start()
    copies[0].wait()
    copies[1].wait()
    pieces = (ids_ref[...].astype(F32).astype(BF16),) + three_pieces(weight_ref[...])
    rows = lax.broadcasted_iota(jnp.int32, (TOP, META), 0)
    lanes = lax.broadcasted_iota(jnp.int32, (TOP, META), 1)
    meta = jnp.zeros((TOK, META), F32)
    for i, piece in enumerate(pieces):
        place = jnp.where(lanes == rows + i * TOP, 1.0, 0.0).astype(BF16)
        meta = meta + dot(piece, place, 0, 0)
    out_ref[:, 2 * D :] = meta.astype(BF16)
    copies[2].wait()
    copies[3].wait()


def pack(tokens, out_grad, ids_t, weight_t):
    return pl.pallas_call(
        pack_kernel,
        out_shape=jax.ShapeDtypeStruct((TOK, COLS), BF16),
        in_specs=[pl.BlockSpec(memory_space=pltpu.HBM)] * 4,
        out_specs=VMEM,
        scratch_shapes=[
            pltpu.VMEM((TOP, TOK), jnp.int32),
            pltpu.VMEM((TOP, TOK), F32),
            pltpu.SemaphoreType.DMA((4,)),
        ],
        compiler_params=params(63),
        name="pack_rows",
    )(tokens, out_grad, ids_t, weight_t)


def hold_kernel(gate_hbm, up_hbm, both_ref, sems):
    copies = [
        pltpu.make_async_copy(gate_hbm.at[0], both_ref.at[:, pl.ds(0, HALF)], sems.at[0]),
        pltpu.make_async_copy(up_hbm.at[0], both_ref.at[:, pl.ds(HALF, HALF)], sems.at[1]),
    ]
    for copy in copies:
        copy.start()
    for copy in copies:
        copy.wait()


def hold(gate_weight, up_weight):
    return pl.pallas_call(
        hold_kernel,
        out_shape=jax.ShapeDtypeStruct((D, 2 * HALF), BF16),
        in_specs=[pl.BlockSpec(memory_space=pltpu.HBM)] * 2,
        out_specs=VMEM,
        scratch_shapes=[pltpu.SemaphoreType.DMA((2,))],
        compiler_params=params(16),
        name="hold_weights",
    )(gate_weight, up_weight)


def spread_kernel(first_ref, *refs):
    blocks, (send_ref, all_ref, mask_ref, weight_ref) = refs[:BLOCKS], refs[BLOCKS:]
    for j, block in enumerate(blocks[:-1]):
        all_ref[min(j, PLANES - 1) * TOK : min(j, PLANES - 1) * TOK + TOK, : block.shape[1]] = block[...]
    all_ref[GROUP - TOK :, D:] = blocks[-1][...]
    meta = all_ref[:, 2 * D :].astype(F32)
    shape = (GROUP, ROWS)
    lane = lax.broadcasted_iota(jnp.int32, shape, 1)
    row = lax.broadcasted_iota(jnp.int32, shape, 0)
    expert = (first_ref[0] + lane // (PLANES * SLOTS)).astype(F32)
    named = jnp.zeros(shape, F32)
    weight = jnp.zeros(shape, F32)
    for k in range(TOP):
        hit = meta[:, k : k + 1] == expert
        w = meta[:, TOP + k : TOP + k + 1] + meta[:, 2 * TOP + k : 2 * TOP + k + 1]
        w = w + meta[:, 3 * TOP + k : 3 * TOP + k + 1]
        named = jnp.where(hit, 1.0, named)
        weight = jnp.where(hit, w, weight)
    ri = lax.broadcasted_iota(jnp.int32, (GROUP, GROUP), 0)
    ci = lax.broadcasted_iota(jnp.int32, (GROUP, GROUP), 1)
    earlier = jnp.where((ri // TOK == ci // TOK) & (ci < ri), 1.0, 0.0).astype(BF16)
    slot = dot(earlier, named.astype(BF16), 1, 0)
    wanted = (lane % SLOTS).astype(F32)
    source = (lane // SLOTS) % PLANES
    mask = jnp.where((slot == wanted) & (source == row // TOK), named, 0.0)
    weight = weight * mask
    mask_ref[...] = mask.astype(BF16)
    weight_ref[...] = weight
    pick = mask.T.astype(BF16)
    scale = jnp.sum(weight.T, axis=1, keepdims=True)
    for i in range(0, D, 512):
        picked = dot(pick, all_ref[:, i : i + 512], 1, 0)
        send_ref[:, :SENT, i : i + 512] = picked.astype(BF16).reshape(CHIPS, SENT, 512)
        picked = dot(pick, all_ref[:, D + i : D + i + 512], 1, 0) * scale
        send_ref[:, SENT:, i : i + 512] = picked.astype(BF16).reshape(CHIPS, SENT, 512)


def spread(first, blocks):
    return pl.pallas_call(
        spread_kernel,
        out_shape=(
            jax.ShapeDtypeStruct((CHIPS, 2 * SENT, D), BF16),
            jax.ShapeDtypeStruct((GROUP, COLS), BF16),
            jax.ShapeDtypeStruct((GROUP, ROWS), BF16),
            jax.ShapeDtypeStruct((GROUP, ROWS), F32),
        ),
        in_specs=[SMEM] + [VMEM] * BLOCKS,
        out_specs=(VMEM,) * 4,
        compiler_params=params(10),
        name="spread_rows",
    )(first, *blocks)


def forward_kernel(in_ref, both_ref, down_ref, back_ref, hidden_ref, gate_out, up_out):
    rows = in_ref[...]
    gate = dot(rows, both_ref[:, :HALF], 1, 0)
    up = dot(rows, both_ref[:, HALF:], 1, 0)
    gate_out[...] = gate
    up_out[...] = up
    hidden = (gate * jax.nn.sigmoid(gate) * up).astype(BF16)
    hidden_ref[...] = hidden
    for i in range(0, D, 1024):
        back_ref[:, i : i + 1024] = dot(hidden, down_ref[0, :, i : i + 1024], 1, 0).astype(BF16)


def backward_kernel(in_ref, gate_in, up_in, both_ref, down_ref, back_ref, pre_ref):
    gate = gate_in[...]
    sig = jax.nn.sigmoid(gate)
    hidden_grad = dot(in_ref[...], down_ref[0], 1, 1)
    pre_ref[:, :HALF] = (hidden_grad * up_in[...] * sig * (1.0 + gate * (1.0 - sig))).astype(BF16)
    pre_ref[:, HALF:] = (hidden_grad * gate * sig).astype(BF16)
    for i in range(0, D, 1024):
        back_ref[:, i : i + 1024] = dot(pre_ref[...], both_ref[i : i + 1024, :], 1, 1).astype(BF16)


COST = pl.CostEstimate(flops=6 * ROWS * D * HALF, bytes_accessed=5 * 2**20, transcendentals=ROWS * HALF)
WIDE = jax.ShapeDtypeStruct((ROWS, D), BF16)
ACT = jax.ShapeDtypeStruct((ROWS, HALF), BF16)
ACT32 = jax.ShapeDtypeStruct((ROWS, HALF), F32)


def forward(rows, weights):
    return pl.pallas_call(
        forward_kernel,
        out_shape=(WIDE, ACT, ACT32, ACT32),
        in_specs=[VMEM] * 3,
        out_specs=(VMEM,) * 4,
        compiler_params=params(16),
        cost_estimate=COST,
        name="forward_rows",
    )(rows, *weights)


def backward(rows, gate, up, weights):
    return pl.pallas_call(
        backward_kernel,
        out_shape=(WIDE, jax.ShapeDtypeStruct((ROWS, 2 * HALF), BF16)),
        in_specs=[VMEM] * 5,
        out_specs=(VMEM,) * 2,
        compiler_params=params(16),
        cost_estimate=COST,
        name="backward_rows",
    )(rows, gate, up, *weights)


def pair_sum_kernel(out_a, out_b, grad_a, grad_b, sum_ref):
    for begin, a_ref, b_ref in ((0, out_a, out_b), (SENT, grad_a, grad_b)):
        total = a_ref[...].astype(F32) + b_ref[...].astype(F32)
        sum_ref[:, begin : begin + SENT, :] = total.astype(BF16).reshape(CHIPS, SENT, D)


def pair_sum(*parts):
    return pl.pallas_call(
        pair_sum_kernel,
        out_shape=jax.ShapeDtypeStruct((CHIPS, 2 * SENT, D), BF16),
        in_specs=[VMEM] * 4,
        out_specs=VMEM,
        compiler_params=params(12),
        name="sum_halves",
    )(*parts)


def weight_grad_kernel(x_a, g_a, x_b, g_b, h_a, p_a, h_b, p_b, gate_ref, up_ref, down_ref):
    both = dot(x_a[...], p_a[...], 0, 0) + dot(x_b[...], p_b[...], 0, 0)
    gate_ref[0] = both[:, :HALF].astype(BF16)
    up_ref[0] = both[:, HALF:].astype(BF16)
    down_ref[0] = (dot(h_a[...], g_a[...], 0, 0) + dot(h_b[...], g_b[...], 0, 0)).astype(BF16)


def weight_grads(own_rows, own_grads, other_rows, other_grads, own_acts, other_acts):
    width = 512
    steps = D // width
    x_spec = pl.BlockSpec((ROWS, width), lambda i: (0, i))
    acts = [pl.BlockSpec((ROWS, HALF), lambda i: (0, 0)), pl.BlockSpec((ROWS, 2 * HALF), lambda i: (0, 0))]
    wide = pl.BlockSpec((1, width, HALF), lambda i: (0, i, 0))
    return pl.pallas_call(
        weight_grad_kernel,
        grid=(steps,),
        out_shape=(
            jax.ShapeDtypeStruct((1, D, HALF), BF16),
            jax.ShapeDtypeStruct((1, D, HALF), BF16),
            jax.ShapeDtypeStruct((1, HALF, D), BF16),
        ),
        in_specs=[x_spec] * 4 + acts + acts,
        out_specs=(wide, wide, pl.BlockSpec((1, HALF, width), lambda i: (0, 0, i))),
        compiler_params=params(20),
        cost_estimate=pl.CostEstimate(
            flops=12 * ROWS * D * HALF, bytes_accessed=12 * 2**20, transcendentals=0
        ),
        name="weight_grads",
    )(own_rows, own_grads, other_rows, other_grads, *own_acts, *other_acts)


def combine_kernel(first_ref, back_ref, all_ref, mask_ref, weight_ref, *out_refs):
    own, below2, above2, down_pair, up_pair, half, other_half = out_refs
    places = ((own, 0), (down_pair, TOK), (up_pair, TOK), (below2, 0), (above2, 0), (down_pair, 0), (up_pair, 0))

    def put(value, begin):
        value = value.astype(BF16)
        end = begin + value.shape[1]
        for j, (ref, row) in enumerate(places):
            ref[row : row + TOK, begin:end] = value[j * TOK : (j + 1) * TOK]
        if begin < D:
            half[:, begin:end] = value[GROUP - TOK :]
        else:
            other_half[:, begin - D : end - D] = value[GROUP - TOK :]

    mask = mask_ref[...]
    weight = weight_ref[...]
    high = weight.astype(BF16)
    low = (weight - high.astype(F32)).astype(BF16)
    both = jnp.concatenate([high, low], axis=0)
    products = jnp.zeros((GROUP, ROWS), F32)
    for i in range(0, D, 512):
        part = back_ref[:, :SENT, i : i + 512].reshape(ROWS, 512)
        total = dot(both, part, 1, 0)
        put(total[:GROUP] + total[GROUP:], i)
        products = products + dot(all_ref[:, D + i : D + i + 512], part, 1, 1)
        put(dot(mask, back_ref[:, SENT:, i : i + 512].reshape(ROWS, 512), 1, 0), D + i)
    meta = all_ref[:, 2 * D :].astype(F32)
    products = products * mask.astype(F32)
    lane = lax.broadcasted_iota(jnp.int32, (GROUP, ROWS), 1)
    expert_of = (first_ref[0] + lane // (PLANES * SLOTS)).astype(F32)
    place = lax.broadcasted_iota(jnp.int32, (GROUP, META), 1)
    tail = jnp.zeros((GROUP, META), F32)
    for k in range(TOP):
        hit = meta[:, k : k + 1] == expert_of
        value = jnp.sum(jnp.where(hit, products, 0.0), axis=1, keepdims=True)
        for i, piece in enumerate(three_pieces(value)):
            tail = jnp.where(place == i * TOP + k, piece.astype(F32), tail)
    put(tail, 2 * D)


def combine(first, back, gathered, mask, weight):
    block = jax.ShapeDtypeStruct((TOK, COLS), BF16)
    pair = jax.ShapeDtypeStruct((2 * TOK, COLS), BF16)
    halves = (jax.ShapeDtypeStruct((TOK, D), BF16), jax.ShapeDtypeStruct((TOK, COLS - D), BF16))
    return pl.pallas_call(
        combine_kernel,
        out_shape=(block, block, block, pair, pair) + halves,
        in_specs=[SMEM] + [VMEM] * 4,
        out_specs=(VMEM,) * 7,
        compiler_params=params(10),
        name="combine_rows",
    )(first, back, gathered, mask, weight)


def relay_kernel(mine_up, next_up, first_half, mine_down, next_down, second_half, up_ref, down_ref):
    up = mine_up[...].astype(F32) + next_up[:TOK].astype(F32)
    up_ref[:, D:] = up[:, D:].astype(BF16)
    up_ref[:, :D] = (up[:, :D] + first_half[...].astype(F32)).astype(BF16)
    down = mine_down[...].astype(F32) + next_down[:TOK].astype(F32)
    down_ref[:, :D] = down[:, :D].astype(BF16)
    down_ref[:, D:] = (down[:, D:] + second_half[...].astype(F32)).astype(BF16)


def relay(*parts):
    block = jax.ShapeDtypeStruct((TOK, COLS), BF16)
    return pl.pallas_call(
        relay_kernel,
        out_shape=(block, block),
        in_specs=[VMEM] * 6,
        out_specs=(VMEM, VMEM),
        compiler_params=params(4),
        name="relay_rows",
    )(*parts)


def total_kernel(*refs):
    *in_refs, out_ref, grad_ref, route_ref = refs
    total = in_refs[0][...].astype(F32)
    for ref in in_refs[1:]:
        total = total + ref[ref.shape[0] - TOK :].astype(F32)
    out_ref[...] = total[:, :D].astype(BF16)
    grad_ref[...] = total[:, D : 2 * D].astype(BF16)
    tail = total[:, 2 * D :].T
    route_ref[...] = tail[:TOP] + tail[TOP : 2 * TOP] + tail[2 * TOP : 3 * TOP]


def totals(*parts):
    return pl.pallas_call(
        total_kernel,
        out_shape=(
            jax.ShapeDtypeStruct((TOK, D), BF16),
            jax.ShapeDtypeStruct((TOK, D), BF16),
            jax.ShapeDtypeStruct((TOP, TOK), F32),
        ),
        in_specs=[VMEM] * len(parts),
        out_specs=(VMEM, VMEM, VMEM),
        compiler_params=params(4),
        name="total_rows",
    )(*parts)


def swap_cores(value):
    return lax.ppermute(value, "core", [(0, 1), (1, 0)])


def over_plane(blocks):
    return lax.all_to_all(blocks, ("y", "x"), 0, 0, tiled=True)


def shift(value, step):
    return lax.ppermute(value, "z", [(i, (i + step) % PLANES) for i in range(PLANES)])


def spread_z(own, weights):
    below2, above2 = shift(own, 2), shift(own, -2)
    below, above = shift(own, 1), shift(own, -1)
    above2, held = lax.optimization_barrier((above2, hold(*weights)))
    half, other_half = shift(below2[:, :D], 2), shift(above2[:, D:], -2)
    below3, above3 = shift(below2, 1), shift(above2, -1)
    return (own, below, above, below2, above2, below3, above3, half, other_half), held


def reduce_z(own, below2, above2, down_pair, up_pair, half, other_half, beside):
    from_above, from_below = shift(down_pair, -1), shift(up_pair, 1)
    half, other_half = shift(half, 2), shift(other_half, -2)
    half, other_half, beside = lax.optimization_barrier((half, other_half, beside))
    up, down = relay(above2, from_below, half, below2, from_above, other_half)
    return totals(own, from_above, from_below, shift(up, 2), shift(down, -2)), beside


def body(tokens, expert_ids, route_weight, out_grad, gate_weight, up_weight, down_weight):
    first = (lax.axis_index("z") * CHIPS).astype(jnp.int32).reshape(1)
    first, tokens = lax.optimization_barrier((first, tokens))
    packed = pack(tokens, out_grad, expert_ids.T, route_weight.T)
    blocks, both = spread_z(packed, (gate_weight, up_weight))
    weights = (both, down_weight)
    send, gathered, mask, weight = spread(first, blocks)
    arrived = over_plane(send)
    rows = arrived[:, :SENT].reshape(ROWS, D)
    grads = arrived[:, SENT:].reshape(ROWS, D)
    other_rows, other_grads = swap_cores(rows), swap_cores(grads)
    out_a, hidden_a, gate_a, up_a = forward(rows, weights)
    hidden_a, other_rows = lax.optimization_barrier((hidden_a, other_rows))
    out_b, hidden_b, gate_b, up_b = forward(other_rows, weights)
    grad_b, pre_b = backward(other_grads, gate_b, up_b, weights)
    from_b, gate_a = lax.optimization_barrier((swap_cores(out_b), gate_a))
    grad_a, pre_a = backward(grads, gate_a, up_a, weights)
    summed = pair_sum(out_a, from_b, grad_a, swap_cores(grad_b))
    back = over_plane(summed)
    back, pre_a = lax.optimization_barrier((back, pre_a))
    weight_out = weight_grads(rows, grads, other_rows, other_grads, (hidden_a, pre_a), (hidden_b, pre_b))
    (layer_out, token_grad, route_t), weight_out = reduce_z(
        *combine(first, back, gathered, mask, weight), beside=weight_out
    )
    return layer_out, token_grad, route_t.T, *weight_out


def solution(mesh):
    fine = Mesh(mesh.devices.reshape(SIZES), AXES)
    rows, pieces = P(AXES, None), P(AXES, None, None)
    return jax.shard_map(
        body,
        mesh=fine,
        in_specs=(rows, rows, rows, rows, pieces, pieces, pieces),
        out_specs=(rows, rows, rows, pieces, pieces, pieces),
        check_vma=False,
    )
```
